32 devices in a mesh: expert: 16 (over z, x, core), dp: 2 (over y).
Axes of the slice: x: 2, y: 2, z: 4, core: 2. Of those that a mesh axis runs over, the one named last changes fastest.
Arguments:
- tokens: bfloat16 [4096, 2048], P(('expert', 'dp')), may hold values from -6 to 6
- upstream: bfloat16 [4096, 2048], P(('expert', 'dp')), may hold values from -6 to 6
- expert_ids: int32 [4096, 2], P(('expert', 'dp')), may hold values from 0 to 15, all different within a row; in each aligned block of 128 rows (0 to 127, 128 to 255, ...) at most 32 rows name the same one
- route_weight: bfloat16 [4096, 2], P(('expert', 'dp')), may hold values from 0.099609375 to 1
- placement: int32 [16], replicated, may hold values from 0 to 15, each once
- swap_pair: int32 [8], replicated, may hold values 0 or 1
- expert_state: bfloat16 [16, 2048, 1024], P('expert', 'dp'), may hold values from -0.125 to 0.125
- first_moment: bfloat16 [16, 2048, 1024], P('expert', 'dp'), may hold values from -60 to 60
- second_moment: bfloat16 [16, 2048, 1024], P('expert', 'dp'), may hold values from 10 to 1000
Outputs:
- token_grad: bfloat16 [4096, 2048], P(('expert', 'dp'))
- weight_grad: bfloat16 [4096, 2], P(('expert', 'dp'))
- new_state: bfloat16 [16, 2048, 1024], P('expert', 'dp')
- new_first: bfloat16 [16, 2048, 1024], P('expert', 'dp')
- new_second: bfloat16 [16, 2048, 1024], P('expert', 'dp')
The draws below stay inside these ranges and needn't reach their ends.
Inputs may be any that keep to these rules, and one draw needn't show every extreme that they name: `expert_ids`: among the rows of one device no expert is named by more than 32 routes, and some expert reaches 32; a token's 2 experts differ.
All inputs are finite; a program needn't handle non-finite values.
Results may differ from the reference program's by a relative error of at most 0.0075.
Values may be sent and summed in bfloat16 or wider, within the bound.
No kernel may reach another device: no remote copies, remote signals or barrier semaphores. Data moves between devices by JAX's collectives and lax.ppermute only.
A program may use at most 64 MiB of HBM per device.

```python
import math
import jax
import jax.numpy as jnp
import numpy as np
from jax import lax

D = 2048
FF = 512
TOK_DEV = 128
TOPK = 2
EXPERTS = 16
CAP = 32
TOKENS = 4096
N_EXPERT = 16
N_DP = 2


def plant(array, key, smallest, high):
    longest = array.shape.index(max(array.shape))
    spots = []
    for shift in (0, 1):
        where = [jax.random.randint(jax.random.fold_in(key, axis), (), 0, length) for axis, length in enumerate(array.shape)]
        where[longest] = (where[longest] + shift) % array.shape[longest]
        spots.append(tuple(where))
    return array.at[spots[0]].set(smallest).at[spots[1]].set(high)


def block_levels(key, dims, shards, smallest, largest):
    def one(dim, shards_of):
        steps = jax.random.uniform(jax.random.fold_in(jax.random.fold_in(key, 6), dim), (shards_of,), jnp.float32, smallest / len(shards), largest / len(shards))
        return jnp.repeat(jnp.exp(steps), dims[dim] // shards_of).reshape((-1,) + (1,) * (len(dims) - dim - 1))

    level = one(*shards[0])
    for cut in shards[1:]:
        level = level * one(*cut)
    return level


def deal_out(key, own, number, rows, number_of, top, reach, lean):
    ranking = jax.random.permutation(key, number_of)
    crowded, ordinary = load_shares(number_of, rows * top, reach, lean, True), load_shares(number_of, rows * top, reach, lean, False)
    places = jnp.arange(number_of)

    def named(tallies, offset_by):
        used = int((tallies > 0).sum())
        fixed = max(1, used // 4)
        passed = fixed + (places - fixed + offset_by * (used - fixed)) % max(1, number_of - fixed)
        return jnp.zeros((number_of,), jnp.int32).at[ranking[jnp.where(places < fixed, places, passed)]].set(jnp.asarray(tallies, jnp.int32))

    tallies = jnp.where(number % 4 == 0, named(crowded, number // 4), named(ordinary, number - number // 4 - 1))
    mixed = jax.random.permutation(jax.random.fold_in(own, 3), number_of)
    source_of, receiver = mixed[0:number_of // 2 * 2:2], mixed[1:number_of // 2 * 2:2]
    slack = jnp.minimum(tallies[source_of] - 1, reach - tallies[receiver]) // 2
    slack = jnp.where((source_of == ranking[0]) | (receiver == ranking[0]) | (tallies[receiver] == 0), 0, jnp.maximum(slack, 0))
    passed = jax.random.randint(jax.random.fold_in(own, 4), (number_of // 2,), 0, 1 << 20) % (slack + 1)
    tallies = tallies.at[source_of].add(-passed).at[receiver].add(passed)
    items = jnp.searchsorted(jnp.cumsum(tallies), jnp.arange(rows * top), side="right").astype(jnp.int32)
    table = items.reshape(top, rows).T
    table = table[jax.random.permutation(jax.random.fold_in(own, 1), rows)]
    offset_by = jax.random.randint(jax.random.fold_in(own, 2), (rows, 1), 0, top)
    return jnp.take_along_axis(table, (jnp.arange(top)[None, :] + offset_by) % top, axis=1)


def load_shares(amount, total, limit, skew, full):
    weights = [(1 << 20) // math.isqrt(rank ** skew) + 1 for rank in range(1, amount + 1)]
    largest = limit if full else min(limit, max(-(-total // amount), total * weights[0] // sum(weights)))
    least = 1 if total - largest >= amount - 1 else 0
    holding, surplus = [largest] + [least] * (amount - 1), total - largest - least * (amount - 1)
    while surplus > 0:
        free = [i for i in range(1, amount) if holding[i] < largest] or [i for i in range(1, amount) if holding[i] < limit]
        pool, budget = sum([weights[i] for i in free]), surplus
        for i in free:
            more = min(limit - holding[i], max(1, budget * weights[i] // pool), surplus)
            holding[i] = holding[i] + more
            surplus = surplus - more
    return np.array(holding)


def normal_values(own_key, dims, scale, most, pieces=(), kind=jnp.bfloat16):
    array = scale * jax.random.normal(own_key, dims, jnp.float32)
    if pieces:
        array = array * block_levels(own_key, dims, pieces, -0.22, 0.18)
    return jnp.clip(array, -most, most).astype(kind)


def setup_inputs(seed: int = 0) -> dict:
    key_of = jax.random.split(jax.random.key(seed), 10)
    tokens = normal_values(key_of[0], (TOKENS, D), 1.0, 6.0, ((0, 32),))
    upstream = normal_values(key_of[1], (TOKENS, D), 1.0, 6.0, ((0, 32),))
    expert_ids_keys = jax.random.split(jax.random.fold_in(key_of[2], 1), TOKENS // TOK_DEV)
    expert_ids_turns = jax.random.permutation(jax.random.fold_in(key_of[2], 3), TOKENS // TOK_DEV)
    expert_ids = jax.vmap(lambda own, number: deal_out(jax.random.fold_in(key_of[2], 2), own, number, TOK_DEV, EXPERTS, TOPK, CAP, 2))(expert_ids_keys, expert_ids_turns).reshape((TOKENS, TOPK))
    route_weight = jnp.clip(jnp.exp(math.log(1.0) - 2.306499 * jax.random.uniform(key_of[3], (TOKENS, TOPK), jnp.float32) ** block_levels(key_of[3], (TOKENS, TOPK), ((0, 32),), -0.2, 0.2)), 0.099609375, 1.0).astype(jnp.bfloat16)
    placement = jax.random.permutation(key_of[4], EXPERTS).astype(jnp.int32)
    swap_pair = plant((jax.random.randint(key_of[5], (EXPERTS // 2,), 0, 2) < 1).astype(jnp.int32), jax.random.fold_in(key_of[5], 1), 0, 1)
    expert_state = normal_values(key_of[6], (EXPERTS, D, 2 * FF), D ** -0.5, 0.125, ((0, 16), (1, 2)))
    first_moment = normal_values(key_of[7], (EXPERTS, D, 2 * FF), 10.0, 60.0, ((0, 16), (1, 2)))
    second_moment = jnp.clip(jnp.exp(math.log(1000.0) - 4.6051702 * jax.random.uniform(key_of[8], (EXPERTS, D, 2 * FF), jnp.float32) ** block_levels(key_of[8], (EXPERTS, D, 2 * FF), ((0, 16), (1, 2)), -0.2, 0.2)), 10.0, 1000.0).astype(jnp.bfloat16)
    return {"tokens": tokens, "upstream": upstream, "expert_ids": expert_ids, "route_weight": route_weight, "placement": placement, "swap_pair": swap_pair, "expert_state": expert_state, "first_moment": first_moment, "second_moment": second_moment}


def silu_grad(value):
    sig = jax.nn.sigmoid(value)
    return sig * (1.0 + value * (1.0 - sig))

def reference(tokens, upstream, expert_ids, route_weight, placement, swap_pair, expert_state, first_moment, second_moment):
    f32 = jnp.float32
    bf16 = jnp.bfloat16
    half = N_EXPERT // 2
    lanes = jnp.arange(N_EXPERT, dtype=jnp.int32)
    source = jnp.where(swap_pair[lanes % half] == 1, lanes ^ half, lanes)
    state_now = expert_state[source]
    first_now = first_moment[source]
    second_now = second_moment[source]
    home = jnp.where(swap_pair[placement % half] == 1, placement ^ half, placement)
    routes = TOK_DEV * TOPK
    ids = expert_ids.reshape(N_EXPERT, N_DP, routes)
    onehot = (ids[..., None] == lanes[None, None, None, :]).astype(jnp.int32)
    slot = lax.optimization_barrier(jnp.sum((jnp.cumsum(onehot, 2) - onehot) * onehot, 3)).astype(jnp.int32)
    dest = home[ids]
    src = jnp.broadcast_to(jnp.arange(N_EXPERT, dtype=jnp.int32)[:, None, None], ids.shape)
    dp_idx = jnp.broadcast_to(jnp.arange(N_DP, dtype=jnp.int32)[None, :, None], ids.shape)
    local = jnp.broadcast_to(jnp.arange(routes, dtype=jnp.int32)[None, None, :], ids.shape)
    route_id = ((src * N_DP + dp_idx) * routes + local).astype(jnp.int32)
    total = TOKENS * TOPK
    table = jnp.full((N_EXPERT, N_DP, N_EXPERT * CAP), total, jnp.int32)
    table = table.at[dest, dp_idx, src * CAP + slot].set(route_id)
    zero_row = jnp.zeros((1, D), bf16)
    route_x = jnp.concatenate([jnp.repeat(tokens, TOPK, axis=0), zero_row], 0)
    route_y = jnp.concatenate([jnp.repeat(upstream, TOPK, axis=0), zero_row], 0)
    route_w = jnp.concatenate([route_weight.reshape(-1), jnp.zeros((1,), bf16)], 0)
    corr_one = 1.0 - math.exp(1000.0 * math.log(0.9))
    corr_two = 1.0 - math.exp(1000.0 * math.log(0.999))

    def per_slot(carry, j):
        dx_all, dw_all = carry
        index = table[j]
        xrows = route_x[index].astype(f32)
        yrows = route_y[index]
        wrows = route_w[index]
        full = state_now[j].astype(f32)
        w_up = full[:, :FF]
        w_down = full[:, FF:]
        hid = jnp.einsum('dmk,kf->dmf', xrows, w_up)
        act = jax.nn.silu(hid).astype(bf16)
        out = jnp.einsum('dmf,kf->dmk', act.astype(f32), w_down)
        slot_dw = lax.optimization_barrier(jnp.sum(yrows.astype(f32) * out, -1)).astype(bf16)
        grad_rows = (wrows.astype(f32)[..., None] * yrows.astype(f32)).astype(bf16)
        back = jnp.einsum('dmk,kf->dmf', grad_rows.astype(f32), w_down)
        dh = (back * silu_grad(hid)).astype(bf16)
        slot_dx = jnp.einsum('dmf,kf->dmk', dh.astype(f32), w_up).astype(bf16)
        g_up = jnp.einsum('dmk,dmf->dkf', xrows, dh.astype(f32))
        g_down = jnp.einsum('dmk,dmf->dkf', grad_rows.astype(f32), act.astype(f32))
        parts = jnp.concatenate([g_up, g_down], -1).astype(bf16)
        grad = lax.optimization_barrier(jnp.sum(parts.astype(f32), 0))
        m2 = 0.9 * first_now[j].astype(f32) + 0.1 * grad
        v2 = 0.999 * second_now[j].astype(f32) + 0.001 * grad * grad
        upd = m2 / corr_one / (jnp.sqrt(v2 / corr_two) + 1e-08)
        w_old = state_now[j].astype(f32)
        w_new = w_old - 0.001 * (upd + 0.1 * w_old)
        flat = index.reshape(-1)
        dx_all = dx_all.at[flat].set(slot_dx.reshape(-1, D))
        dw_all = dw_all.at[flat].set(slot_dw.reshape(-1))
        return ((dx_all, dw_all), (w_new.astype(bf16), m2.astype(bf16), v2.astype(bf16)))
    init = (jnp.zeros((total + 1, D), bf16), jnp.zeros((total + 1,), bf16))
    (dx_all, dw_all), (new_state, new_first, new_second) = lax.scan(per_slot, init, jnp.arange(N_EXPERT, dtype=jnp.int32))
    token_grad = lax.optimization_barrier(jnp.sum(dx_all[:total].reshape(TOKENS, TOPK, D).astype(f32), 1)).astype(bf16)
    weight_grad = dw_all[:total].reshape(TOKENS, TOPK)
    return (token_grad, weight_grad, new_state, new_first, new_second)
```

```python
import math

import jax
import jax.numpy as jnp
from jax import lax
from jax.sharding import PartitionSpec as P

corr_one = 1.0 - math.exp(1000.0 * math.log(0.9))
corr_two = 1.0 - math.exp(1000.0 * math.log(0.999))

f32 = jnp.float32
bf16 = jnp.bfloat16


def silu_grad(value):
    sig = jax.nn.sigmoid(value)
    return sig * (1.0 + value * (1.0 - sig))


def adam_update(weights, first, second, grad):
    m_next = 0.9 * first.astype(f32) + 0.1 * grad
    v_next = 0.999 * second.astype(f32) + 0.001 * grad * grad
    update = m_next / corr_one / (jnp.sqrt(v_next / corr_two) + 1e-08)
    w_old = weights.astype(f32)
    w_next = w_old - 0.001 * (update + 0.1 * w_old)
    return w_next.astype(bf16), m_next.astype(bf16), v_next.astype(bf16)


def trade(arrays, swap_pair):
    lanes_count = lax.axis_size("expert")
    half = lanes_count // 2
    groups = min(half, 8)
    members = half // groups
    flags = (jnp.max(swap_pair.reshape(groups, members), 1) == 1).astype(jnp.int32)
    traded = arrays
    for column in range(2):
        own_groups = [group for group in range(groups) if (group >> 1) & 1 == column]
        pattern = sum(flags[group] << bit for bit, group in enumerate(own_groups))

        def branch(bits):
            moving = [group for bit, group in enumerate(own_groups) if (bits >> bit) & 1]
            pairs = [
                (slot ^ half if (slot % half) // members in moving else slot, slot)
                for slot in range(lanes_count)
            ]

            def run(*values):
                if bits == 0:
                    return values
                return tuple(lax.ppermute(value, "expert", pairs) for value in values)

            return run

        traded = lax.switch(pattern, [branch(bits) for bits in range(2 ** len(own_groups))], *traded)
    if members > 1:
        own = lax.axis_index("expert") % half
        own_flag = jnp.sum(jnp.where(jnp.arange(half) == own, swap_pair, 0))
        traded = tuple(jnp.where(own_flag == 1, new, old) for new, old in zip(traded, arrays))
    return traded


def shards(
    tokens,
    upstream,
    expert_ids,
    route_weight,
    placement,
    swap_pair,
    expert_state,
    first_moment,
    second_moment,
):
    lanes_count = lax.axis_size("expert")
    n_dp = lax.axis_size("dp")
    rows, top = expert_ids.shape
    width = tokens.shape[1]
    hidden_units = expert_state.shape[2] // 2
    capacity = 2 * rows * top // lanes_count
    slots = lanes_count * capacity
    part = width // n_dp
    dp = lax.axis_index("dp")

    def exchange(value):
        return lax.all_to_all(
            value.reshape(lanes_count, capacity, -1), "expert", split_axis=0, concat_axis=0, tiled=True
        ).reshape(slots, -1)

    def shift(value, step):
        return lax.ppermute(value, "dp", [(i, (i + step) % n_dp) for i in range(n_dp)])

    state = expert_state[0]
    pieces = [state] + [shift(state, step) for step in range(1, n_dp)]
    starts = [((dp - step) % n_dp) * part for step in range(n_dp)]

    def columns(value, step):
        return lax.dynamic_slice_in_dim(value, starts[step], part, 1)

    ids = expert_ids.T
    same = (ids[:, :, None] == expert_ids[None, None, :, 0]) | (
        ids[:, :, None] == expert_ids[None, None, :, 1]
    )
    time = jnp.arange(rows)
    slot = jnp.sum((same & (time[None, None, :] < time[None, :, None])).astype(jnp.int32), 2)
    lanes = jnp.arange(lanes_count, dtype=jnp.int32)
    dest = jnp.sum(jnp.where(ids[:, :, None] == lanes, placement, 0), 2)
    position = dest * capacity + slot
    hot = (jnp.arange(slots, dtype=jnp.int32)[None, :, None] == position[:, None, :]).astype(bf16)
    both = jnp.sum(hot, 0)
    weighted = jnp.sum(hot * route_weight.T[:, None, :], 0)

    x_rows = exchange(jnp.dot(both, tokens, preferred_element_type=f32).astype(bf16))
    g_rows = exchange(jnp.dot(weighted, upstream, preferred_element_type=f32).astype(bf16))

    def up(step):
        return pieces[step][:, :hidden_units]

    def down(step):
        return pieces[step][:, hidden_units:]

    hid = sum(
        jnp.dot(columns(x_rows, s), up(s), preferred_element_type=f32) for s in range(n_dp)
    )
    act = jax.nn.silu(hid).astype(bf16)
    back = sum(
        jnp.dot(columns(g_rows, s), down(s), preferred_element_type=f32) for s in range(n_dp)
    )
    dh = (back * silu_grad(hid)).astype(bf16)
    slot_dw = jnp.sum(act.astype(f32) * back, 1)

    def grad_part(step):
        both_sides = [
            lax.dot_general(columns(a, step), b, (((0,), (0,)), ((), ())), preferred_element_type=f32)
            for a, b in ((x_rows, dh), (g_rows, act))
        ]
        return jnp.concatenate(both_sides, 1).astype(bf16)

    received = [shift(grad_part(step), n_dp - step) for step in range(1, n_dp)]
    dx = [
        lax.dot_general(dh, up(s), (((1,), (1,)), ((), ())), preferred_element_type=f32).astype(bf16)
        for s in range(n_dp)
    ]
    dx_all = jnp.zeros((slots, width + 128), bf16)
    for step in range(n_dp):
        dx_all = lax.dynamic_update_slice(dx_all, dx[step], (0, starts[step]))
    dx_all = lax.dynamic_update_slice(
        dx_all, jnp.broadcast_to(slot_dw[:, None], (slots, 128)).astype(bf16), (0, width)
    )
    returned = exchange(dx_all)
    token_grad = lax.dot_general(
        both, returned[:, :width], (((0,), (0,)), ((), ())), preferred_element_type=f32
    ).astype(bf16)
    dw_cols = lax.dot_general(
        hot, returned[:, width:], (((1,), (0,)), ((), ())), preferred_element_type=f32
    )
    weight_grad = (dw_cols[:, :, 0].T / route_weight.astype(f32)).astype(bf16)

    grad = grad_part(0).astype(f32)
    for value in received:
        grad = grad + value.astype(f32)
    updated = adam_update(state, first_moment[0], second_moment[0], grad)
    w2, m2, v2 = trade(updated, swap_pair)
    return (token_grad, weight_grad, w2[None], m2[None], v2[None])


def solution(mesh):
    in_specs = (
        P(("expert", "dp"), None),
        P(("expert", "dp"), None),
        P(("expert", "dp"), None),
        P(("expert", "dp"), None),
        P(),
        P(),
        P("expert", "dp", None),
        P("expert", "dp", None),
        P("expert", "dp", None),
    )
    out_specs = (
        P(("expert", "dp"), None),
        P(("expert", "dp"), None),
        P("expert", "dp", None),
        P("expert", "dp", None),
        P("expert", "dp", None),
    )
    return jax.shard_map(shards, mesh=mesh, in_specs=in_specs, out_specs=out_specs, check_vma=False)
```

```python
import math

import jax
import jax.numpy as jnp
from jax import lax
from jax.sharding import PartitionSpec as P

corr_one = 1.0 - math.exp(1000.0 * math.log(0.9))
corr_two = 1.0 - math.exp(1000.0 * math.log(0.999))

f32 = jnp.float32
bf16 = jnp.bfloat16


def silu_grad(value):
    sig = jax.nn.sigmoid(value)
    return sig * (1.0 + value * (1.0 - sig))


def adam_update(weights, first, second, grad):
    m_next = 0.9 * first.astype(f32) + 0.1 * grad
    v_next = 0.999 * second.astype(f32) + 0.001 * grad * grad
    update = m_next / corr_one / (jnp.sqrt(v_next / corr_two) + 1e-08)
    w_old = weights.astype(f32)
    w_next = w_old - 0.001 * (update + 0.1 * w_old)
    return w_next.astype(bf16), m_next.astype(bf16), v_next.astype(bf16)


def trade(arrays, swap_pair):
    lanes_count = lax.axis_size("expert")
    half = lanes_count // 2
    own = lax.axis_index("expert") % half
    own_flag = jnp.sum(jnp.where(jnp.arange(half, dtype=jnp.int32) == own, swap_pair, 0))
    pairs = [(slot ^ half, slot) for slot in range(lanes_count)]

    def swap(*values):
        return tuple(lax.ppermute(value, "expert", pairs) for value in values)

    return lax.cond(own_flag == 1, swap, lambda *values: values, *arrays)


def shards(
    tokens,
    upstream,
    expert_ids,
    route_weight,
    placement,
    swap_pair,
    expert_state,
    first_moment,
    second_moment,
):
    lanes_count = lax.axis_size("expert")
    n_dp = lax.axis_size("dp")
    rows, top = expert_ids.shape
    width = tokens.shape[1]
    hidden_units = expert_state.shape[2] // 2
    capacity = 2 * rows * top // lanes_count
    slots = lanes_count * capacity
    part = width // n_dp
    dp = lax.axis_index("dp")

    def exchange(value):
        return lax.all_to_all(
            value.reshape(lanes_count, capacity, -1), "expert", split_axis=0, concat_axis=0, tiled=True
        ).reshape(slots, -1)

    def shift(value, step):
        return lax.ppermute(value, "dp", [(i, (i + step) % n_dp) for i in range(n_dp)])

    state = expert_state[0]
    pieces = [state] + [shift(state, step) for step in range(1, n_dp)]
    starts = [((dp - step) % n_dp) * part for step in range(n_dp)]

    def columns(value, step):
        return lax.dynamic_slice_in_dim(value, starts[step], part, 1)

    ids = expert_ids.T
    same = (ids[:, :, None] == expert_ids[None, None, :, 0]) | (
        ids[:, :, None] == expert_ids[None, None, :, 1]
    )
    time = jnp.arange(rows)
    slot = jnp.sum((same & (time[None, None, :] < time[None, :, None])).astype(jnp.int32), 2)
    lanes = jnp.arange(lanes_count, dtype=jnp.int32)
    dest = jnp.sum(jnp.where(ids[:, :, None] == lanes, placement, 0), 2)
    position = dest * capacity + slot
    hot = (jnp.arange(slots, dtype=jnp.int32)[None, :, None] == position[:, None, :]).astype(bf16)
    both = jnp.sum(hot, 0)
    weighted = jnp.sum(hot * route_weight.T[:, None, :], 0)

    x_rows = exchange(jnp.dot(both, tokens, preferred_element_type=f32).astype(bf16))
    g_rows = exchange(jnp.dot(weighted, upstream, preferred_element_type=f32).astype(bf16))

    def up(step):
        return pieces[step][:, :hidden_units]

    def down(step):
        return pieces[step][:, hidden_units:]

    hid = sum(
        jnp.dot(columns(x_rows, s), up(s), preferred_element_type=f32) for s in range(n_dp)
    )
    act = jax.nn.silu(hid).astype(bf16)
    back = sum(
        jnp.dot(columns(g_rows, s), down(s), preferred_element_type=f32) for s in range(n_dp)
    )
    dh = (back * silu_grad(hid)).astype(bf16)
    slot_dw = jnp.sum(act.astype(f32) * back, 1)

    def grad_part(step):
        both_sides = [
            lax.dot_general(columns(a, step), b, (((0,), (0,)), ((), ())), preferred_element_type=f32)
            for a, b in ((x_rows, dh), (g_rows, act))
        ]
        return jnp.concatenate(both_sides, 1).astype(bf16)

    received = [shift(grad_part(step), n_dp - step) for step in range(1, n_dp)]
    dx = [
        lax.dot_general(dh, up(s), (((1,), (1,)), ((), ())), preferred_element_type=f32).astype(bf16)
        for s in range(n_dp)
    ]
    dx_all = jnp.zeros((slots, width + 128), bf16)
    for step in range(n_dp):
        dx_all = lax.dynamic_update_slice(dx_all, dx[step], (0, starts[step]))
    dx_all = lax.dynamic_update_slice(
        dx_all, jnp.broadcast_to(slot_dw[:, None], (slots, 128)).astype(bf16), (0, width)
    )
    returned = exchange(dx_all)
    token_grad = lax.dot_general(
        both, returned[:, :width], (((0,), (0,)), ((), ())), preferred_element_type=f32
    ).astype(bf16)
    dw_cols = lax.dot_general(
        hot, returned[:, width:], (((1,), (0,)), ((), ())), preferred_element_type=f32
    )
    weight_grad = (dw_cols[:, :, 0].T / route_weight.astype(f32)).astype(bf16)

    grad = grad_part(0).astype(f32)
    for value in received:
        grad = grad + value.astype(f32)
    updated = adam_update(state, first_moment[0], second_moment[0], grad)
    w2, m2, v2 = trade(updated, swap_pair)
    return (token_grad, weight_grad, w2[None], m2[None], v2[None])


def solution(mesh):
    in_specs = (
        P(("expert", "dp"), None),
        P(("expert", "dp"), None),
        P(("expert", "dp"), None),
        P(("expert", "dp"), None),
        P(),
        P(),
        P("expert", "dp", None),
        P("expert", "dp", None),
        P("expert", "dp", None),
    )
    out_specs = (
        P(("expert", "dp"), None),
        P(("expert", "dp"), None),
        P("expert", "dp", None),
        P("expert", "dp", None),
        P("expert", "dp", None),
    )
    return jax.shard_map(shards, mesh=mesh, in_specs=in_specs, out_specs=out_specs, check_vma=False)
```

```python
import math

import jax
import jax.numpy as jnp
from jax import lax
from jax.experimental import pallas as pl
from jax.experimental.pallas import tpu as pltpu
from jax.sharding import PartitionSpec as P

corr_one = 1.0 - math.exp(1000.0 * math.log(0.9))
corr_two = 1.0 - math.exp(1000.0 * math.log(0.999))

f32 = jnp.float32
bf16 = jnp.bfloat16


TRANSPOSED = (((0,), (0,)), ((), ()))
BY_ROWS = (((1,), (1,)), ((), ()))


def matmul(a, b, dims=(((1,), (0,)), ((), ()))):
    return lax.dot_general(a, b, dims, preferred_element_type=f32)


def adam_update(weights, first, second, grad):
    m_next = 0.9 * first.astype(f32) + 0.1 * grad
    v_next = 0.999 * second.astype(f32) + 0.001 * grad * grad
    update = m_next / corr_one / (jnp.sqrt(v_next / corr_two) + 1e-08)
    w_old = weights.astype(f32)
    w_next = w_old - 0.001 * (update + 0.1 * w_old)
    return w_next.astype(bf16), m_next.astype(bf16), v_next.astype(bf16)


def dispatch(both, weighted, tokens, upstream):
    slots, rows = both.shape
    width = tokens.shape[1]
    block = 512
    count = width // block

    def kernel(both_ref, weighted_ref, tokens_ref, upstream_ref, out_ref):
        step = pl.program_id(0)

        @pl.when(step < count)
        def _():
            out_ref[...] = matmul(both_ref[...], tokens_ref[...]).astype(bf16)

        @pl.when(step >= count)
        def _():
            out_ref[...] = matmul(weighted_ref[...], upstream_ref[...]).astype(bf16)

    return pl.pallas_call(
        kernel,
        out_shape=jax.ShapeDtypeStruct((slots, 2 * width), bf16),
        grid=(2 * count,),
        in_specs=[
            pl.BlockSpec((slots, rows), lambda i: (0, 0)),
            pl.BlockSpec((slots, rows), lambda i: (0, 0)),
            pl.BlockSpec((rows, block), lambda i: (0, jnp.minimum(i, count - 1))),
            pl.BlockSpec((rows, block), lambda i: (0, jnp.maximum(i - count, 0))),
        ],
        out_specs=pl.BlockSpec((slots, block), lambda i: (0, i)),
        compiler_params=pltpu.CompilerParams(vmem_limit_bytes=32 * 2**20),
        cost_estimate=pl.CostEstimate(
            flops=4 * slots * rows * width, bytes_accessed=5 * slots * width, transcendentals=0
        ),
        name="dispatch",
    )(both, weighted, tokens, upstream)


def expert_step(starts, routed, pieces):
    slots = routed.shape[0]
    width = routed.shape[1] // 2
    n_dp = len(pieces)
    part, both_hidden = pieces[0].shape
    hidden_units = both_hidden // 2
    block = min(256, part)
    count = part // block

    def kernel(starts_ref, x_ref, g_ref, *refs):
        w_refs = refs[:n_dp]
        act_ref, dh_ref, dx_ref = refs[n_dp : n_dp + 3]
        part_refs = refs[n_dp + 3 : 2 * n_dp + 2]
        hid_ref, back_ref = refs[2 * n_dp + 2 :]
        phase, step = pl.program_id(0), pl.program_id(1)
        for piece in range(n_dp):
            here = step // count == piece

            @pl.when(here & (phase == 0))
            def _():
                hid = matmul(x_ref[...], w_refs[piece][:, :hidden_units])
                back = matmul(g_ref[...], w_refs[piece][:, hidden_units:])
                if piece == 0:
                    @pl.when(step == 0)
                    def _():
                        hid_ref[...] = hid
                        back_ref[...] = back

                    @pl.when(step > 0)
                    def _():
                        hid_ref[...] += hid
                        back_ref[...] += back
                else:
                    hid_ref[...] += hid
                    back_ref[...] += back

            @pl.when(here & (phase == 1))
            def _():
                start = starts_ref[piece] * block + (step - piece * count) * block
                dx_ref[:, pl.ds(pl.multiple_of(start, block), block)] = matmul(
                    dh_ref[...], w_refs[piece][:, :hidden_units], BY_ROWS
                ).astype(bf16)
                if piece > 0:
                    out = part_refs[piece - 1]
                    out[:, :hidden_units] = matmul(x_ref[...], dh_ref[...], TRANSPOSED).astype(bf16)
                    out[:, hidden_units:] = matmul(g_ref[...], act_ref[...], TRANSPOSED).astype(bf16)

        @pl.when((phase == 0) & (step == n_dp * count - 1))
        def _():
            hid, back = hid_ref[...], back_ref[...]
            sig = jax.nn.sigmoid(hid)
            act = (hid * sig).astype(bf16)
            act_ref[...] = act
            dh_ref[...] = (back * (sig * (1.0 + hid * (1.0 - sig)))).astype(bf16)
            dw = jnp.sum(act.astype(f32) * back, 1, keepdims=True)
            dx_ref[:, width:] = jnp.broadcast_to(dw, (slots, 128)).astype(bf16)

    def column(first):
        def index(phase, step, starts_ref):
            return (0, first + starts_ref[step // count] + step % count)

        return index

    def of_piece(piece):
        return lambda phase, step, _: (jnp.clip(step - piece * count, 0, count - 1), 0)

    def of_part(piece):
        return lambda phase, step, _: (jnp.clip(step - piece * count, 0, count - 1) * phase, 0)

    def whole(phase, step, _):
        return (0, 0)

    return pl.pallas_call(
        kernel,
        out_shape=[
            jax.ShapeDtypeStruct((slots, hidden_units), bf16),
            jax.ShapeDtypeStruct((slots, hidden_units), bf16),
            jax.ShapeDtypeStruct((slots, width + 128), bf16),
        ]
        + [jax.ShapeDtypeStruct((part, both_hidden), bf16)] * (n_dp - 1),
        grid_spec=pltpu.PrefetchScalarGridSpec(
            num_scalar_prefetch=1,
            grid=(2, n_dp * count),
            in_specs=[
                pl.BlockSpec((slots, block), column(0)),
                pl.BlockSpec((slots, block), column(width // block)),
            ]
            + [pl.BlockSpec((block, both_hidden), of_piece(piece)) for piece in range(n_dp)],
            out_specs=[
                pl.BlockSpec((slots, hidden_units), whole),
                pl.BlockSpec((slots, hidden_units), whole),
                pl.BlockSpec((slots, width + 128), whole),
            ]
            + [pl.BlockSpec((block, both_hidden), of_part(piece)) for piece in range(1, n_dp)],
            scratch_shapes=[pltpu.VMEM((slots, hidden_units), f32)] * 2,
        ),
        compiler_params=pltpu.CompilerParams(vmem_limit_bytes=48 * 2**20),
        cost_estimate=pl.CostEstimate(
            flops=10 * slots * width * hidden_units,
            bytes_accessed=24 * slots * width,
            transcendentals=slots * hidden_units,
        ),
        name="expert_step",
    )(starts // block, routed, routed, *pieces)


def gradient_and_adam(start, routed, act, dh, received, state, first, second):
    slots = routed.shape[0]
    width = routed.shape[1] // 2
    part, both_hidden = state.shape[1:]
    hidden_units = both_hidden // 2
    block = min(256, part)

    def kernel(start_ref, x_ref, g_ref, act_ref, dh_ref, *refs):
        part_refs = refs[: len(received)]
        w_ref, m_ref, v_ref, w2_ref, m2_ref, v2_ref = refs[len(received) :]
        for half, (rows_ref, other_ref) in enumerate(((x_ref, dh_ref), (g_ref, act_ref))):
            cols = slice(half * hidden_units, (half + 1) * hidden_units)
            grad = matmul(rows_ref[...], other_ref[...], TRANSPOSED).astype(bf16).astype(f32)
            for part_ref in part_refs:
                grad = grad + part_ref[:, cols].astype(f32)
            new = adam_update(w_ref[0, :, cols], m_ref[0, :, cols], v_ref[0, :, cols], grad)
            for ref, value in zip((w2_ref, m2_ref, v2_ref), new):
                ref[0, :, cols] = value

    state_spec = pl.BlockSpec((1, block, both_hidden), lambda i, _: (0, i, 0))
    part_spec = pl.BlockSpec((block, both_hidden), lambda i, _: (i, 0))
    whole_spec = pl.BlockSpec((slots, hidden_units), lambda i, _: (0, 0))
    return pl.pallas_call(
        kernel,
        out_shape=[jax.ShapeDtypeStruct(state.shape, bf16)] * 3,
        grid_spec=pltpu.PrefetchScalarGridSpec(
            num_scalar_prefetch=1,
            grid=(part // block,),
            in_specs=[
                pl.BlockSpec((slots, block), lambda i, start_ref: (0, start_ref[0] + i)),
                pl.BlockSpec(
                    (slots, block), lambda i, start_ref: (0, width // block + start_ref[0] + i)
                ),
                whole_spec,
                whole_spec,
            ]
            + [part_spec] * len(received)
            + [state_spec] * 3,
            out_specs=[state_spec] * 3,
        ),
        compiler_params=pltpu.CompilerParams(vmem_limit_bytes=48 * 2**20),
        cost_estimate=pl.CostEstimate(
            flops=4 * slots * part * hidden_units,
            bytes_accessed=20 * part * both_hidden,
            transcendentals=2 * part * both_hidden,
        ),
        name="gradient_and_adam",
    )(start // block, routed, routed, act, dh, *received, state, first, second)


def trade(arrays, swap_pair):
    lanes_count = lax.axis_size("expert")
    half = lanes_count // 2
    own = lax.axis_index("expert") % half
    own_flag = jnp.sum(jnp.where(jnp.arange(half, dtype=jnp.int32) == own, swap_pair, 0))
    pairs = [(slot ^ half, slot) for slot in range(lanes_count)]

    def swap(*values):
        return tuple(lax.ppermute(value, "expert", pairs) for value in values)

    return lax.cond(own_flag == 1, swap, lambda *values: values, *arrays)


def shards(
    tokens,
    upstream,
    expert_ids,
    route_weight,
    placement,
    swap_pair,
    expert_state,
    first_moment,
    second_moment,
):
    lanes_count = lax.axis_size("expert")
    n_dp = lax.axis_size("dp")
    rows, top = expert_ids.shape
    width = tokens.shape[1]
    hidden_units = expert_state.shape[2] // 2
    capacity = 2 * rows * top // lanes_count
    slots = lanes_count * capacity
    part = width // n_dp
    dp = lax.axis_index("dp")

    def exchange(value):
        return lax.all_to_all(
            value.reshape(lanes_count, capacity, -1), "expert", split_axis=0, concat_axis=0, tiled=True
        ).reshape(slots, -1)

    def shift(value, step):
        return lax.ppermute(value, "dp", [(i, (i + step) % n_dp) for i in range(n_dp)])

    state = expert_state[0]
    pieces = [state] + [shift(state, step) for step in range(1, n_dp)]
    starts = ((dp - jnp.arange(n_dp, dtype=jnp.int32)) % n_dp) * part

    ids = expert_ids.T
    same = (ids[:, :, None] == expert_ids[None, None, :, 0]) | (
        ids[:, :, None] == expert_ids[None, None, :, 1]
    )
    time = jnp.arange(rows)
    slot = jnp.sum((same & (time[None, None, :] < time[None, :, None])).astype(jnp.int32), 2)
    lanes = jnp.arange(lanes_count, dtype=jnp.int32)
    dest = jnp.sum(jnp.where(ids[:, :, None] == lanes, placement, 0), 2)
    position = dest * capacity + slot
    hot = (jnp.arange(slots, dtype=jnp.int32)[None, :, None] == position[:, None, :]).astype(bf16)
    both = jnp.sum(hot, 0)
    weighted = jnp.sum(hot * route_weight.T[:, None, :], 0)

    routed = exchange(dispatch(both, weighted, tokens, upstream))
    act, dh, dx, *parts = expert_step(starts, routed, pieces)
    received = [shift(value, n_dp - step) for step, value in enumerate(parts, 1)]
    returned = exchange(dx)
    token_grad = matmul(both, returned[:, :width], TRANSPOSED).astype(bf16)
    dw_cols = matmul(hot, returned[:, width:], (((1,), (0,)), ((), ())))
    weight_grad = (dw_cols[:, :, 0].T / route_weight.astype(f32)).astype(bf16)

    updated = gradient_and_adam(
        starts[:1], routed, act, dh, received, expert_state, first_moment, second_moment
    )
    token_grad, weight_grad, *updated = lax.optimization_barrier(
        (token_grad, weight_grad, *updated)
    )
    return (token_grad, weight_grad, *trade(updated, swap_pair))


def solution(mesh):
    in_specs = (
        P(("expert", "dp"), None),
        P(("expert", "dp"), None),
        P(("expert", "dp"), None),
        P(("expert", "dp"), None),
        P(),
        P(),
        P("expert", "dp", None),
        P("expert", "dp", None),
        P("expert", "dp", None),
    )
    out_specs = (
        P(("expert", "dp"), None),
        P(("expert", "dp"), None),
        P("expert", "dp", None),
        P("expert", "dp", None),
        P("expert", "dp", None),
    )
    return jax.shard_map(shards, mesh=mesh, in_specs=in_specs, out_specs=out_specs, check_vma=False)
```

```python
import math

import jax
import jax.numpy as jnp
from jax import lax
from jax.experimental import pallas as pl
from jax.experimental.pallas import tpu as pltpu
from jax.sharding import PartitionSpec as P

corr_one = 1.0 - math.exp(1000.0 * math.log(0.9))
corr_two = 1.0 - math.exp(1000.0 * math.log(0.999))

f32 = jnp.float32
bf16 = jnp.bfloat16


TRANSPOSED = (((0,), (0,)), ((), ()))
BY_ROWS = (((1,), (1,)), ((), ()))


def matmul(a, b, dims=(((1,), (0,)), ((), ()))):
    return lax.dot_general(a, b, dims, preferred_element_type=f32)


def adam_update(weights, first, second, grad):
    m_next = 0.9 * first.astype(f32) + 0.1 * grad
    v_next = 0.999 * second.astype(f32) + 0.001 * grad * grad
    update = m_next / corr_one / (jnp.sqrt(v_next / corr_two) + 1e-08)
    w_old = weights.astype(f32)
    w_next = w_old - 0.001 * (update + 0.1 * w_old)
    return w_next.astype(bf16), m_next.astype(bf16), v_next.astype(bf16)


def dispatch(both, weighted, tokens, upstream):
    slots, rows = both.shape
    width = tokens.shape[1]
    block = 512
    count = width // block

    def kernel(both_ref, weighted_ref, tokens_ref, upstream_ref, out_ref):
        step = pl.program_id(0)

        @pl.when(step < count)
        def _():
            out_ref[...] = matmul(both_ref[...], tokens_ref[...]).astype(bf16)

        @pl.when(step >= count)
        def _():
            out_ref[...] = matmul(weighted_ref[...], upstream_ref[...]).astype(bf16)

    return pl.pallas_call(
        kernel,
        out_shape=jax.ShapeDtypeStruct((slots, 2 * width), bf16),
        grid=(2 * count,),
        in_specs=[
            pl.BlockSpec((slots, rows), lambda i: (0, 0)),
            pl.BlockSpec((slots, rows), lambda i: (0, 0)),
            pl.BlockSpec((rows, block), lambda i: (0, jnp.minimum(i, count - 1))),
            pl.BlockSpec((rows, block), lambda i: (0, jnp.maximum(i - count, 0))),
        ],
        out_specs=pl.BlockSpec((slots, block), lambda i: (0, i)),
        compiler_params=pltpu.CompilerParams(vmem_limit_bytes=32 * 2**20),
        cost_estimate=pl.CostEstimate(
            flops=4 * slots * rows * width, bytes_accessed=5 * slots * width, transcendentals=0
        ),
        name="dispatch",
    )(both, weighted, tokens, upstream)


def expert_step(starts, routed, pieces):
    slots = routed.shape[0]
    width = routed.shape[1] // 2
    n_dp = len(pieces)
    part, both_hidden = pieces[0].shape
    hidden_units = both_hidden // 2
    block = min(512, part)
    count = part // block

    def kernel(starts_ref, x_ref, g_ref, *refs):
        w_refs = refs[:n_dp]
        act_ref, dh_ref, dx_ref = refs[n_dp : n_dp + 3]
        part_refs = refs[n_dp + 3 : 2 * n_dp + 2]
        hid_ref, back_ref = refs[2 * n_dp + 2 :]
        phase, step = pl.program_id(0), pl.program_id(1)
        for piece in range(n_dp):
            here = step // count == piece

            @pl.when(here & (phase == 0))
            def _():
                hid = matmul(x_ref[...], w_refs[piece][:, :hidden_units])
                back = matmul(g_ref[...], w_refs[piece][:, hidden_units:])
                if piece == 0:
                    @pl.when(step == 0)
                    def _():
                        hid_ref[...] = hid
                        back_ref[...] = back

                    @pl.when(step > 0)
                    def _():
                        hid_ref[...] += hid
                        back_ref[...] += back
                else:
                    hid_ref[...] += hid
                    back_ref[...] += back

            @pl.when(here & (phase == 1))
            def _():
                start = starts_ref[piece] * block + (step - piece * count) * block
                dx_ref[:, pl.ds(pl.multiple_of(start, block), block)] = matmul(
                    dh_ref[...], w_refs[piece][:, :hidden_units], BY_ROWS
                ).astype(bf16)
                if piece > 0:
                    out = part_refs[piece - 1]
                    out[:, :hidden_units] = matmul(x_ref[...], dh_ref[...], TRANSPOSED).astype(bf16)
                    out[:, hidden_units:] = matmul(g_ref[...], act_ref[...], TRANSPOSED).astype(bf16)

        @pl.when((phase == 0) & (step == n_dp * count - 1))
        def _():
            hid, back = hid_ref[...], back_ref[...]
            sig = jax.nn.sigmoid(hid)
            act = (hid * sig).astype(bf16)
            act_ref[...] = act
            dh_ref[...] = (back * (sig * (1.0 + hid * (1.0 - sig)))).astype(bf16)
            dw = jnp.sum(act.astype(f32) * back, 1, keepdims=True)
            dx_ref[:, width:] = jnp.broadcast_to(dw, (slots, 128)).astype(bf16)

    def column(first):
        def index(phase, step, starts_ref):
            return (0, first + starts_ref[step // count] + step % count)

        return index

    def of_piece(piece):
        return lambda phase, step, _: (jnp.clip(step - piece * count, 0, count - 1), 0)

    def of_part(piece):
        return lambda phase, step, _: (jnp.clip(step - piece * count, 0, count - 1) * phase, 0)

    def whole(phase, step, _):
        return (0, 0)

    return pl.pallas_call(
        kernel,
        out_shape=[
            jax.ShapeDtypeStruct((slots, hidden_units), bf16),
            jax.ShapeDtypeStruct((slots, hidden_units), bf16),
            jax.ShapeDtypeStruct((slots, width + 128), bf16),
        ]
        + [jax.ShapeDtypeStruct((part, both_hidden), bf16)] * (n_dp - 1),
        grid_spec=pltpu.PrefetchScalarGridSpec(
            num_scalar_prefetch=1,
            grid=(2, n_dp * count),
            in_specs=[
                pl.BlockSpec((slots, block), column(0)),
                pl.BlockSpec((slots, block), column(width // block)),
            ]
            + [pl.BlockSpec((block, both_hidden), of_piece(piece)) for piece in range(n_dp)],
            out_specs=[
                pl.BlockSpec((slots, hidden_units), whole),
                pl.BlockSpec((slots, hidden_units), whole),
                pl.BlockSpec((slots, width + 128), whole),
            ]
            + [pl.BlockSpec((block, both_hidden), of_part(piece)) for piece in range(1, n_dp)],
            scratch_shapes=[pltpu.VMEM((slots, hidden_units), f32)] * 2,
        ),
        compiler_params=pltpu.CompilerParams(vmem_limit_bytes=48 * 2**20),
        cost_estimate=pl.CostEstimate(
            flops=10 * slots * width * hidden_units,
            bytes_accessed=24 * slots * width,
            transcendentals=slots * hidden_units,
        ),
        name="expert_step",
    )(starts // block, routed, routed, *pieces)


def gradient_and_adam(start, routed, act, dh, received, state, first, second):
    slots = routed.shape[0]
    width = routed.shape[1] // 2
    part, both_hidden = state.shape[1:]
    hidden_units = both_hidden // 2
    block = min(256, part)

    def kernel(start_ref, x_ref, g_ref, act_ref, dh_ref, *refs):
        part_refs = refs[: len(received)]
        w_ref, m_ref, v_ref, w2_ref, m2_ref, v2_ref = refs[len(received) :]
        for half, (rows_ref, other_ref) in enumerate(((x_ref, dh_ref), (g_ref, act_ref))):
            cols = slice(half * hidden_units, (half + 1) * hidden_units)
            grad = matmul(rows_ref[...], other_ref[...], TRANSPOSED).astype(bf16).astype(f32)
            for part_ref in part_refs:
                grad = grad + part_ref[:, cols].astype(f32)
            new = adam_update(w_ref[0, :, cols], m_ref[0, :, cols], v_ref[0, :, cols], grad)
            for ref, value in zip((w2_ref, m2_ref, v2_ref), new):
                ref[0, :, cols] = value

    state_spec = pl.BlockSpec((1, block, both_hidden), lambda i, _: (0, i, 0))
    part_spec = pl.BlockSpec((block, both_hidden), lambda i, _: (i, 0))
    whole_spec = pl.BlockSpec((slots, hidden_units), lambda i, _: (0, 0))
    return pl.pallas_call(
        kernel,
        out_shape=[jax.ShapeDtypeStruct(state.shape, bf16)] * 3,
        grid_spec=pltpu.PrefetchScalarGridSpec(
            num_scalar_prefetch=1,
            grid=(part // block,),
            in_specs=[
                pl.BlockSpec((slots, block), lambda i, start_ref: (0, start_ref[0] + i)),
                pl.BlockSpec(
                    (slots, block), lambda i, start_ref: (0, width // block + start_ref[0] + i)
                ),
                whole_spec,
                whole_spec,
            ]
            + [part_spec] * len(received)
            + [state_spec] * 3,
            out_specs=[state_spec] * 3,
        ),
        compiler_params=pltpu.CompilerParams(vmem_limit_bytes=48 * 2**20),
        cost_estimate=pl.CostEstimate(
            flops=4 * slots * part * hidden_units,
            bytes_accessed=20 * part * both_hidden,
            transcendentals=2 * part * both_hidden,
        ),
        name="gradient_and_adam",
    )(start // block, routed, routed, act, dh, *received, state, first, second)


def trade(arrays, swap_pair, beside, operands):
    lanes_count = lax.axis_size("expert")
    half = lanes_count // 2
    own = lax.axis_index("expert") % half
    lanes = jnp.arange(half, dtype=jnp.int32)
    own_flag = jnp.sum(jnp.where(lanes == own, swap_pair, 0))
    other_flag = jnp.sum(jnp.where(lanes == own ^ 2, swap_pair, 0))
    side = (own >> 1) & 1
    rows = arrays[0].shape[1]
    cut = rows * 9 // 16

    def permute(value, pairs):
        return lax.ppermute(value, "expert", pairs)

    def stay(values, operands):
        return values, beside(*operands)

    def both(values, operands):
        pairs = [(slot ^ half, slot) for slot in range(lanes_count)]
        return tuple(permute(value, pairs) for value in values), beside(*operands)

    def one(trading):
        def run(values, operands):
            mine = [slot for slot in range(lanes_count) if (slot >> 1) & 1 == trading]
            across = [(slot ^ half, slot) for slot in mine]
            aside = [(slot, slot ^ 2) for slot in mine]
            across_aside = [(slot ^ half ^ 2, slot ^ 2) for slot in mine]
            back = [(slot ^ 2, slot) for slot in mine]
            last = [permute(value[:, cut:], aside) for value in values]
            first = [permute(value[:, :cut], across) for value in values]
            last = [permute(value, across_aside) for value in last]
            last = [permute(value, back) for value in last]
            traded = tuple(
                jnp.where(side == trading, jnp.concatenate([top, bottom], 1), value)
                for top, bottom, value in zip(first, last, values)
            )
            return traded, beside(*operands)

        return run

    if half < 4:
        return lax.cond(own_flag == 1, both, stay, arrays, operands)
    pattern = jnp.where(own_flag == 1, jnp.where(other_flag == 1, 3, 1 + side), 0)
    pattern = jnp.where((own_flag == 0) & (other_flag == 1), 2 - side, pattern)
    return lax.switch(pattern, [stay, one(0), one(1), both], arrays, operands)


def shards(
    tokens,
    upstream,
    expert_ids,
    route_weight,
    placement,
    swap_pair,
    expert_state,
    first_moment,
    second_moment,
):
    lanes_count = lax.axis_size("expert")
    n_dp = lax.axis_size("dp")
    rows, top = expert_ids.shape
    width = tokens.shape[1]
    hidden_units = expert_state.shape[2] // 2
    capacity = 2 * rows * top // lanes_count
    slots = lanes_count * capacity
    part = width // n_dp
    dp = lax.axis_index("dp")

    def exchange(value):
        return lax.all_to_all(
            value.reshape(lanes_count, capacity, -1), "expert", split_axis=0, concat_axis=0, tiled=True
        ).reshape(slots, -1)

    def shift(value, step):
        return lax.ppermute(value, "dp", [(i, (i + step) % n_dp) for i in range(n_dp)])

    state = expert_state[0]
    pieces = [state] + [shift(state, step) for step in range(1, n_dp)]
    starts = ((dp - jnp.arange(n_dp, dtype=jnp.int32)) % n_dp) * part

    ids = expert_ids.T
    same = (ids[:, :, None] == expert_ids[None, None, :, 0]) | (
        ids[:, :, None] == expert_ids[None, None, :, 1]
    )
    time = jnp.arange(rows)
    slot = jnp.sum((same & (time[None, None, :] < time[None, :, None])).astype(jnp.int32), 2)
    lanes = jnp.arange(lanes_count, dtype=jnp.int32)
    dest = jnp.sum(jnp.where(ids[:, :, None] == lanes, placement, 0), 2)
    position = dest * capacity + slot
    hot = (jnp.arange(slots, dtype=jnp.int32)[None, :, None] == position[:, None, :]).astype(bf16)
    both = jnp.sum(hot, 0)
    weighted = jnp.sum(hot * route_weight.T[:, None, :], 0)

    routed = exchange(dispatch(both, weighted, tokens, upstream))
    act, dh, dx, *parts = expert_step(starts, routed, pieces)
    received = [shift(value, n_dp - step) for step, value in enumerate(parts, 1)]
    returned = exchange(dx)
    updated = gradient_and_adam(
        starts[:1], routed, act, dh, received, expert_state, first_moment, second_moment
    )

    def combine(returned, both, hot, route_weight):
        token_grad = matmul(both, returned[:, :width], TRANSPOSED).astype(bf16)
        dw_cols = matmul(hot, returned[:, width:], (((1,), (0,)), ((), ())))
        return token_grad, (dw_cols[:, :, 0].T / route_weight.astype(f32)).astype(bf16)

    updated, gradients = trade(
        tuple(updated), swap_pair, combine, (returned, both, hot, route_weight)
    )
    return (*gradients, *updated)


def solution(mesh):
    in_specs = (
        P(("expert", "dp"), None),
        P(("expert", "dp"), None),
        P(("expert", "dp"), None),
        P(("expert", "dp"), None),
        P(),
        P(),
        P("expert", "dp", None),
        P("expert", "dp", None),
        P("expert", "dp", None),
    )
    out_specs = (
        P(("expert", "dp"), None),
        P(("expert", "dp"), None),
        P("expert", "dp", None),
        P("expert", "dp", None),
        P("expert", "dp", None),
    )
    return jax.shard_map(shards, mesh=mesh, in_specs=in_specs, out_specs=out_specs, check_vma=False)
```

```python
import math

import jax
import jax.numpy as jnp
from jax import lax
from jax.experimental import pallas as pl
from jax.experimental.pallas import tpu as pltpu
from jax.sharding import PartitionSpec as P

corr_one = 1.0 - math.exp(1000.0 * math.log(0.9))
corr_two = 1.0 - math.exp(1000.0 * math.log(0.999))

f32 = jnp.float32
bf16 = jnp.bfloat16


TRANSPOSED = (((0,), (0,)), ((), ()))
BY_ROWS = (((1,), (1,)), ((), ()))


def matmul(a, b, dims=(((1,), (0,)), ((), ()))):
    return lax.dot_general(a, b, dims, preferred_element_type=f32)


def adam_update(weights, first, second, grad):
    m_next = 0.9 * first.astype(f32) + 0.1 * grad
    v_next = 0.999 * second.astype(f32) + 0.001 * grad * grad
    root = v_next * (1.0 / corr_two)
    update = m_next * (1.0 / corr_one) / (root * lax.rsqrt(root) + 1e-08)
    w_old = weights.astype(f32)
    w_next = w_old - 0.001 * (update + 0.1 * w_old)
    return w_next.astype(bf16), m_next.astype(bf16), v_next.astype(bf16)


def dispatch(expert_ids, route_weight, placement, tokens, upstream, capacity):
    top, rows = expert_ids.shape
    lanes_count = placement.shape[0]
    slots = lanes_count * capacity
    width = tokens.shape[1]
    block = 512
    count = width // block

    def kernel(placement_ref, ids_ref, weight_ref, tokens_ref, upstream_ref, out_ref, position_ref, both_ref, weighted_ref):
        step = pl.program_id(0)

        @pl.when(step == 0)
        def _():
            ids = [ids_ref[k : k + 1, :] for k in range(top)]
            spread = [jnp.broadcast_to(row.astype(f32), (rows, rows)) for row in ids]
            earlier = lax.broadcasted_iota(jnp.int32, (rows, rows), 0) < lax.broadcasted_iota(
                jnp.int32, (rows, rows), 1
            )
            place = lax.broadcasted_iota(jnp.int32, (slots, rows), 0)
            both = jnp.zeros((slots, rows), f32)
            weighted = jnp.zeros((slots, rows), f32)
            for k in range(top):
                slot = jnp.zeros((1, rows), f32)
                for other in range(top):
                    same = (spread[other].T == spread[k]) & earlier
                    slot = slot + jnp.sum(jnp.where(same, 1.0, 0.0), 0, keepdims=True)
                dest = jnp.zeros((1, rows), jnp.int32)
                for expert in range(lanes_count):
                    dest = jnp.where(ids[k] == expert, placement_ref[expert], dest)
                position = dest * capacity + slot.astype(jnp.int32)
                position_ref[k : k + 1, :] = position
                hot = place == position
                both = jnp.where(hot, 1.0, both)
                weighted = jnp.where(hot, weight_ref[k : k + 1, :].astype(f32), weighted)
            both_ref[...] = both.astype(bf16)
            weighted_ref[...] = weighted.astype(bf16)

        @pl.when(step < count)
        def _():
            out_ref[...] = matmul(both_ref[...], tokens_ref[...]).astype(bf16)

        @pl.when(step >= count)
        def _():
            out_ref[...] = matmul(weighted_ref[...], upstream_ref[...]).astype(bf16)

    return pl.pallas_call(
        kernel,
        out_shape=[
            jax.ShapeDtypeStruct((slots, 2 * width), bf16),
            jax.ShapeDtypeStruct((top, rows), jnp.int32),
        ],
        grid_spec=pltpu.PrefetchScalarGridSpec(
            num_scalar_prefetch=1,
            grid=(2 * count,),
            in_specs=[
                pl.BlockSpec((top, rows), lambda i, _: (0, 0)),
                pl.BlockSpec((top, rows), lambda i, _: (0, 0)),
                pl.BlockSpec((rows, block), lambda i, _: (0, jnp.minimum(i, count - 1))),
                pl.BlockSpec((rows, block), lambda i, _: (0, jnp.maximum(i - count, 0))),
            ],
            out_specs=[
                pl.BlockSpec((slots, block), lambda i, _: (0, i)),
                pl.BlockSpec((top, rows), lambda i, _: (0, 0)),
            ],
            scratch_shapes=[pltpu.VMEM((slots, rows), bf16)] * 2,
        ),
        compiler_params=pltpu.CompilerParams(vmem_limit_bytes=32 * 2**20),
        cost_estimate=pl.CostEstimate(
            flops=4 * slots * rows * width, bytes_accessed=5 * slots * width, transcendentals=0
        ),
        name="dispatch",
    )(placement, expert_ids, route_weight, tokens, upstream)


def expert_step(starts, routed, pieces):
    slots = routed.shape[0]
    width = routed.shape[1] // 2
    n_dp = len(pieces)
    part, both_hidden = pieces[0].shape
    hidden_units = both_hidden // 2
    block = min(512, part)
    count = part // block
    total = n_dp * count

    def kernel(starts_ref, x_ref, g_ref, *refs):
        w_refs = refs[:n_dp]
        act_ref, dh_ref, dw_ref = refs[n_dp : n_dp + 3]
        part_refs = refs[n_dp + 3 : 2 * n_dp + 2]
        hid_ref, back_ref = refs[2 * n_dp + 2 :]
        step = pl.program_id(0)
        for piece in range(n_dp):

            @pl.when((step >= piece * count) & (step < (piece + 1) * count))
            def _():
                hid = matmul(x_ref[...], w_refs[piece][:, :hidden_units])
                back = matmul(g_ref[...], w_refs[piece][:, hidden_units:])

                @pl.when(step == 0)
                def _():
                    hid_ref[...] = hid
                    back_ref[...] = back

                @pl.when(step > 0)
                def _():
                    hid_ref[...] += hid
                    back_ref[...] += back

            if piece > 0:
                first = total + (piece - 1) * count

                @pl.when((step >= first) & (step < first + count))
                def _():
                    out = part_refs[piece - 1]
                    out[:, :hidden_units] = matmul(x_ref[...], dh_ref[...], TRANSPOSED).astype(bf16)
                    out[:, hidden_units:] = matmul(g_ref[...], act_ref[...], TRANSPOSED).astype(bf16)

        @pl.when(step == total - 1)
        def _():
            hid, back = hid_ref[...], back_ref[...]
            sig = jax.nn.sigmoid(hid)
            act = (hid * sig).astype(bf16)
            act_ref[...] = act
            dh_ref[...] = (back * (sig * (1.0 + hid * (1.0 - sig)))).astype(bf16)
            dw = jnp.sum(act.astype(f32) * back, 1, keepdims=True)
            dw_ref[...] = jnp.broadcast_to(dw, (slots, 128)).astype(bf16)

    def column(first):
        def index(step, starts_ref):
            at = jnp.where(step < total, step, step - total + count)
            return (0, first + starts_ref[at // count] + at % count)

        return index

    def of_piece(piece):
        return lambda step, _: (jnp.clip(step - piece * count, 0, count - 1), 0)

    def of_part(piece):
        return lambda step, _: (jnp.clip(step - total - (piece - 1) * count, 0, count - 1), 0)

    def whole(step, _):
        return (0, 0)

    return pl.pallas_call(
        kernel,
        out_shape=[
            jax.ShapeDtypeStruct((slots, hidden_units), bf16),
            jax.ShapeDtypeStruct((slots, hidden_units), bf16),
            jax.ShapeDtypeStruct((slots, 128), bf16),
        ]
        + [jax.ShapeDtypeStruct((part, both_hidden), bf16)] * (n_dp - 1),
        grid_spec=pltpu.PrefetchScalarGridSpec(
            num_scalar_prefetch=1,
            grid=(total + (n_dp - 1) * count,),
            in_specs=[
                pl.BlockSpec((slots, block), column(0)),
                pl.BlockSpec((slots, block), column(width // block)),
            ]
            + [pl.BlockSpec((block, both_hidden), of_piece(piece)) for piece in range(n_dp)],
            out_specs=[
                pl.BlockSpec((slots, hidden_units), whole),
                pl.BlockSpec((slots, hidden_units), whole),
                pl.BlockSpec((slots, 128), whole),
            ]
            + [pl.BlockSpec((block, both_hidden), of_part(piece)) for piece in range(1, n_dp)],
            scratch_shapes=[pltpu.VMEM((slots, hidden_units), f32)] * 2,
        ),
        compiler_params=pltpu.CompilerParams(vmem_limit_bytes=48 * 2**20),
        cost_estimate=pl.CostEstimate(
            flops=8 * slots * width * hidden_units,
            bytes_accessed=16 * slots * width,
            transcendentals=slots * hidden_units,
        ),
        name="expert_step",
    )(starts // block, routed, routed, *pieces)


def input_gradient(starts, dh, dw, pieces):
    slots, hidden_units = dh.shape
    n_dp = len(pieces)
    part = pieces[0].shape[0]
    width = n_dp * part
    block = min(512, part)
    count = part // block

    def kernel(starts_ref, dh_ref, dw_ref, *refs):
        dx_ref = refs[n_dp]
        step = pl.program_id(0)

        @pl.when(step == 0)
        def _():
            dx_ref[:, width:] = dw_ref[...]

        for piece in range(n_dp):

            @pl.when(step // count == piece)
            def _():
                start = (starts_ref[piece] + step - piece * count) * block
                dx_ref[:, pl.ds(pl.multiple_of(start, block), block)] = matmul(
                    dh_ref[...], refs[piece][...], BY_ROWS
                ).astype(bf16)

    def of_piece(piece):
        return lambda step, _: (jnp.clip(step - piece * count, 0, count - 1), 0)

    def whole(step, _):
        return (0, 0)

    return pl.pallas_call(
        kernel,
        out_shape=jax.ShapeDtypeStruct((slots, width + 128), bf16),
        grid_spec=pltpu.PrefetchScalarGridSpec(
            num_scalar_prefetch=1,
            grid=(n_dp * count,),
            in_specs=[
                pl.BlockSpec((slots, hidden_units), whole),
                pl.BlockSpec((slots, 128), whole),
            ]
            + [pl.BlockSpec((block, hidden_units), of_piece(piece)) for piece in range(n_dp)],
            out_specs=pl.BlockSpec((slots, width + 128), whole),
        ),
        compiler_params=pltpu.CompilerParams(vmem_limit_bytes=32 * 2**20),
        cost_estimate=pl.CostEstimate(
            flops=2 * slots * width * hidden_units,
            bytes_accessed=4 * slots * width,
            transcendentals=0,
        ),
        name="input_gradient",
    )(starts // block, dh, dw, *pieces)


def gradient_and_adam(start, routed, act, dh, received, state, first, second):
    slots = routed.shape[0]
    width = routed.shape[1] // 2
    part, both_hidden = state.shape[1:]
    hidden_units = both_hidden // 2
    block = min(256, part)

    def kernel(start_ref, x_ref, g_ref, act_ref, dh_ref, *refs):
        part_refs = refs[: len(received)]
        w_ref, m_ref, v_ref, w2_ref, m2_ref, v2_ref = refs[len(received) :]
        for half, (rows_ref, other_ref) in enumerate(((x_ref, dh_ref), (g_ref, act_ref))):
            cols = slice(half * hidden_units, (half + 1) * hidden_units)
            grad = matmul(rows_ref[...], other_ref[...], TRANSPOSED).astype(bf16).astype(f32)
            for part_ref in part_refs:
                grad = grad + part_ref[:, cols].astype(f32)
            new = adam_update(w_ref[0, :, cols], m_ref[0, :, cols], v_ref[0, :, cols], grad)
            for ref, value in zip((w2_ref, m2_ref, v2_ref), new):
                ref[0, :, cols] = value

    state_spec = pl.BlockSpec((1, block, both_hidden), lambda i, _: (0, i, 0))
    part_spec = pl.BlockSpec((block, both_hidden), lambda i, _: (i, 0))
    whole_spec = pl.BlockSpec((slots, hidden_units), lambda i, _: (0, 0))
    return pl.pallas_call(
        kernel,
        out_shape=[jax.ShapeDtypeStruct(state.shape, bf16)] * 3,
        grid_spec=pltpu.PrefetchScalarGridSpec(
            num_scalar_prefetch=1,
            grid=(part // block,),
            in_specs=[
                pl.BlockSpec((slots, block), lambda i, start_ref: (0, start_ref[0] + i)),
                pl.BlockSpec(
                    (slots, block), lambda i, start_ref: (0, width // block + start_ref[0] + i)
                ),
                whole_spec,
                whole_spec,
            ]
            + [part_spec] * len(received)
            + [state_spec] * 3,
            out_specs=[state_spec] * 3,
        ),
        compiler_params=pltpu.CompilerParams(vmem_limit_bytes=48 * 2**20),
        cost_estimate=pl.CostEstimate(
            flops=4 * slots * part * hidden_units,
            bytes_accessed=20 * part * both_hidden,
            transcendentals=2 * part * both_hidden,
        ),
        name="gradient_and_adam",
    )(start // block, routed, routed, act, dh, *received, state, first, second)


def trade(arrays, swap_pair, beside, operands):
    lanes_count = lax.axis_size("expert")
    half = lanes_count // 2
    own = lax.axis_index("expert") % half
    lanes = jnp.arange(half, dtype=jnp.int32)
    own_flag = jnp.sum(jnp.where(lanes == own, swap_pair, 0))
    other_flag = jnp.sum(jnp.where(lanes == own ^ 2, swap_pair, 0))
    side = (own >> 1) & 1
    rows = arrays[0].shape[1]
    cut = rows * 9 // 16

    def permute(value, pairs):
        return lax.ppermute(value, "expert", pairs)

    def stay(values, operands):
        return values, beside(*operands)

    def both(values, operands):
        pairs = [(slot ^ half, slot) for slot in range(lanes_count)]
        return tuple(permute(value, pairs) for value in values), beside(*operands)

    def one(trading):
        def run(values, operands):
            mine = [slot for slot in range(lanes_count) if (slot >> 1) & 1 == trading]
            across = [(slot ^ half, slot) for slot in mine]
            aside = [(slot, slot ^ 2) for slot in mine]
            across_aside = [(slot ^ half ^ 2, slot ^ 2) for slot in mine]
            back = [(slot ^ 2, slot) for slot in mine]
            last = [permute(value[:, cut:], aside) for value in values]
            first = [permute(value[:, :cut], across) for value in values]
            last = [permute(value, across_aside) for value in last]
            last = [permute(value, back) for value in last]
            traded = tuple(
                jnp.where(side == trading, jnp.concatenate([top, bottom], 1), value)
                for top, bottom, value in zip(first, last, values)
            )
            return traded, beside(*operands)

        return run

    if half < 4:
        return lax.cond(own_flag == 1, both, stay, arrays, operands)
    pattern = jnp.where(own_flag == 1, jnp.where(other_flag == 1, 3, 1 + side), 0)
    pattern = jnp.where((own_flag == 0) & (other_flag == 1), 2 - side, pattern)
    return lax.switch(pattern, [stay, one(0), one(1), both], arrays, operands)


def shards(
    tokens,
    upstream,
    expert_ids,
    route_weight,
    placement,
    swap_pair,
    expert_state,
    first_moment,
    second_moment,
):
    lanes_count = lax.axis_size("expert")
    n_dp = lax.axis_size("dp")
    rows, top = expert_ids.shape
    width = tokens.shape[1]
    hidden_units = expert_state.shape[2] // 2
    capacity = 2 * rows * top // lanes_count
    slots = lanes_count * capacity
    part = width // n_dp
    dp = lax.axis_index("dp")

    def exchange(value):
        return lax.all_to_all(
            value.reshape(lanes_count, capacity, -1), "expert", split_axis=0, concat_axis=0, tiled=True
        ).reshape(slots, -1)

    def shift(value, step):
        return lax.ppermute(value, "dp", [(i, (i + step) % n_dp) for i in range(n_dp)])

    state = expert_state[0]
    pieces = [state] + [shift(state, step) for step in range(1, n_dp)]
    starts = ((dp - jnp.arange(n_dp, dtype=jnp.int32)) % n_dp) * part

    rows_of_slots, position = dispatch(
        expert_ids.T, route_weight.T, placement, tokens, upstream, capacity
    )
    routed = exchange(rows_of_slots)
    act, dh, dw, *parts = expert_step(starts, routed, pieces)
    received = [shift(value, n_dp - step) for step, value in enumerate(parts, 1)]
    returned = exchange(input_gradient(starts, dh, dw, pieces))
    updated = gradient_and_adam(
        starts[:1], routed, act, dh, received, expert_state, first_moment, second_moment
    )

    def combine(returned, position, route_weight):
        slot = jnp.arange(slots, dtype=jnp.int32)
        hot = (slot[None, :, None] == position[:, None, :]).astype(bf16)
        token_grad = matmul(jnp.sum(hot, 0), returned[:, :width], TRANSPOSED).astype(bf16)
        dw_cols = matmul(hot, returned[:, width:], (((1,), (0,)), ((), ())))
        return token_grad, (dw_cols[:, :, 0].T / route_weight.astype(f32)).astype(bf16)

    updated, gradients = trade(
        tuple(updated), swap_pair, combine, (returned, position, route_weight)
    )
    return (*gradients, *updated)


def solution(mesh):
    in_specs = (
        P(("expert", "dp"), None),
        P(("expert", "dp"), None),
        P(("expert", "dp"), None),
        P(("expert", "dp"), None),
        P(),
        P(),
        P("expert", "dp", None),
        P("expert", "dp", None),
        P("expert", "dp", None),
    )
    out_specs = (
        P(("expert", "dp"), None),
        P(("expert", "dp"), None),
        P("expert", "dp", None),
        P("expert", "dp", None),
        P("expert", "dp", None),
    )
    return jax.shard_map(shards, mesh=mesh, in_specs=in_specs, out_specs=out_specs, check_vma=False)
```

```python
import math

import jax
import jax.numpy as jnp
from jax import lax
from jax.experimental import pallas as pl
from jax.experimental.pallas import tpu as pltpu
from jax.sharding import PartitionSpec as P

corr_one = 1.0 - math.exp(1000.0 * math.log(0.9))
corr_two = 1.0 - math.exp(1000.0 * math.log(0.999))

f32 = jnp.float32
bf16 = jnp.bfloat16


TRANSPOSED = (((0,), (0,)), ((), ()))
BY_ROWS = (((1,), (1,)), ((), ()))


def matmul(a, b, dims=(((1,), (0,)), ((), ()))):
    return lax.dot_general(a, b, dims, preferred_element_type=f32)


def adam_update(weights, first, second, grad):
    m_next = 0.9 * first.astype(f32) + 0.1 * grad
    v_next = 0.999 * second.astype(f32) + 0.001 * grad * grad
    root = v_next * (1.0 / corr_two)
    update = m_next * (1.0 / corr_one) / (root * lax.rsqrt(root) + 1e-08)
    w_old = weights.astype(f32)
    w_next = w_old - 0.001 * (update + 0.1 * w_old)
    return w_next.astype(bf16), m_next.astype(bf16), v_next.astype(bf16)


def dispatch(expert_ids, route_weight, placement, tokens, upstream, capacity):
    top, rows = expert_ids.shape
    lanes_count = placement.shape[0]
    slots = lanes_count * capacity
    width = tokens.shape[1]
    block = 512
    count = width // block

    def kernel(placement_ref, ids_ref, weight_ref, tokens_ref, upstream_ref, out_ref, position_ref, both_ref, weighted_ref):
        step = pl.program_id(0)

        @pl.when(step == 0)
        def _():
            ids = [ids_ref[k : k + 1, :] for k in range(top)]
            spread = [jnp.broadcast_to(row.astype(f32), (rows, rows)) for row in ids]
            earlier = lax.broadcasted_iota(jnp.int32, (rows, rows), 0) < lax.broadcasted_iota(
                jnp.int32, (rows, rows), 1
            )
            place = lax.broadcasted_iota(jnp.int32, (slots, rows), 0)
            both = jnp.zeros((slots, rows), f32)
            weighted = jnp.zeros((slots, rows), f32)
            for k in range(top):
                slot = jnp.zeros((1, rows), f32)
                for other in range(top):
                    same = (spread[other].T == spread[k]) & earlier
                    slot = slot + jnp.sum(jnp.where(same, 1.0, 0.0), 0, keepdims=True)
                dest = jnp.zeros((1, rows), jnp.int32)
                for expert in range(lanes_count):
                    dest = jnp.where(ids[k] == expert, placement_ref[expert], dest)
                position = dest * capacity + slot.astype(jnp.int32)
                position_ref[k : k + 1, :] = position
                hot = place == position
                both = jnp.where(hot, 1.0, both)
                weighted = jnp.where(hot, weight_ref[k : k + 1, :].astype(f32), weighted)
            both_ref[...] = both.astype(bf16)
            weighted_ref[...] = weighted.astype(bf16)

        @pl.when(step < count)
        def _():
            out_ref[...] = matmul(both_ref[...], tokens_ref[...]).astype(bf16)

        @pl.when(step >= count)
        def _():
            out_ref[...] = matmul(weighted_ref[...], upstream_ref[...]).astype(bf16)

    return pl.pallas_call(
        kernel,
        out_shape=[
            jax.ShapeDtypeStruct((slots, 2 * width), bf16),
            jax.ShapeDtypeStruct((top, rows), jnp.int32),
        ],
        grid_spec=pltpu.PrefetchScalarGridSpec(
            num_scalar_prefetch=1,
            grid=(2 * count,),
            in_specs=[
                pl.BlockSpec((top, rows), lambda i, _: (0, 0)),
                pl.BlockSpec((top, rows), lambda i, _: (0, 0)),
                pl.BlockSpec((rows, block), lambda i, _: (0, jnp.minimum(i, count - 1))),
                pl.BlockSpec((rows, block), lambda i, _: (0, jnp.maximum(i - count, 0))),
            ],
            out_specs=[
                pl.BlockSpec((slots, block), lambda i, _: (0, i)),
                pl.BlockSpec((top, rows), lambda i, _: (0, 0)),
            ],
            scratch_shapes=[pltpu.VMEM((slots, rows), bf16)] * 2,
        ),
        compiler_params=pltpu.CompilerParams(vmem_limit_bytes=56 * 2**20),
        cost_estimate=pl.CostEstimate(
            flops=4 * slots * rows * width, bytes_accessed=5 * slots * width, transcendentals=0
        ),
        name="dispatch",
    )(placement, expert_ids, route_weight, tokens, upstream)


def expert_step(starts, routed, pieces):
    slots = routed.shape[0]
    width = routed.shape[1] // 2
    n_dp = len(pieces)
    part, both_hidden = pieces[0].shape
    hidden_units = both_hidden // 2
    block = min(512, part)
    count = part // block
    total = n_dp * count

    def kernel(starts_ref, x_ref, g_ref, *refs):
        w_refs = refs[:n_dp]
        act_ref, dh_ref, dw_ref = refs[n_dp : n_dp + 3]
        part_refs = refs[n_dp + 3 : 2 * n_dp + 2]
        hid_ref, back_ref = refs[2 * n_dp + 2 :]
        step = pl.program_id(0)
        for piece in range(n_dp):

            @pl.when((step >= piece * count) & (step < (piece + 1) * count))
            def _():
                hid = matmul(x_ref[...], w_refs[piece][:, :hidden_units])
                back = matmul(g_ref[...], w_refs[piece][:, hidden_units:])

                @pl.when(step == 0)
                def _():
                    hid_ref[...] = hid
                    back_ref[...] = back

                @pl.when(step > 0)
                def _():
                    hid_ref[...] += hid
                    back_ref[...] += back

            if piece > 0:
                first = total + (piece - 1) * count

                @pl.when((step >= first) & (step < first + count))
                def _():
                    out = part_refs[piece - 1]
                    out[:, :hidden_units] = matmul(x_ref[...], dh_ref[...], TRANSPOSED).astype(bf16)
                    out[:, hidden_units:] = matmul(g_ref[...], act_ref[...], TRANSPOSED).astype(bf16)

        @pl.when(step == total - 1)
        def _():
            hid, back = hid_ref[...], back_ref[...]
            sig = jax.nn.sigmoid(hid)
            act = (hid * sig).astype(bf16)
            act_ref[...] = act
            dh_ref[...] = (back * (sig * (1.0 + hid * (1.0 - sig)))).astype(bf16)
            dw = jnp.sum(act.astype(f32) * back, 1, keepdims=True)
            dw_ref[...] = jnp.broadcast_to(dw, (slots, 128)).astype(bf16)

    def column(first):
        def index(step, starts_ref):
            at = jnp.where(step < total, step, step - total + count)
            return (0, first + starts_ref[at // count] + at % count)

        return index

    def of_piece(piece):
        return lambda step, _: (jnp.clip(step - piece * count, 0, count - 1), 0)

    def of_part(piece):
        return lambda step, _: (jnp.clip(step - total - (piece - 1) * count, 0, count - 1), 0)

    def whole(step, _):
        return (0, 0)

    return pl.pallas_call(
        kernel,
        out_shape=[
            jax.ShapeDtypeStruct((slots, hidden_units), bf16),
            jax.ShapeDtypeStruct((slots, hidden_units), bf16),
            jax.ShapeDtypeStruct((slots, 128), bf16),
        ]
        + [jax.ShapeDtypeStruct((part, both_hidden), bf16)] * (n_dp - 1),
        grid_spec=pltpu.PrefetchScalarGridSpec(
            num_scalar_prefetch=1,
            grid=(total + (n_dp - 1) * count,),
            in_specs=[
                pl.BlockSpec((slots, block), column(0)),
                pl.BlockSpec((slots, block), column(width // block)),
            ]
            + [pl.BlockSpec((block, both_hidden), of_piece(piece)) for piece in range(n_dp)],
            out_specs=[
                pl.BlockSpec((slots, hidden_units), whole),
                pl.BlockSpec((slots, hidden_units), whole),
                pl.BlockSpec((slots, 128), whole),
            ]
            + [pl.BlockSpec((block, both_hidden), of_part(piece)) for piece in range(1, n_dp)],
            scratch_shapes=[pltpu.VMEM((slots, hidden_units), f32)] * 2,
        ),
        compiler_params=pltpu.CompilerParams(vmem_limit_bytes=56 * 2**20),
        cost_estimate=pl.CostEstimate(
            flops=8 * slots * width * hidden_units,
            bytes_accessed=16 * slots * width,
            transcendentals=slots * hidden_units,
        ),
        name="expert_step",
    )(starts // block, routed, routed, *pieces)


def input_gradient(starts, dh, dw, pieces):
    slots, hidden_units = dh.shape
    n_dp = len(pieces)
    part = pieces[0].shape[0]
    width = n_dp * part
    block = min(512, part)
    count = part // block

    def kernel(starts_ref, dh_ref, dw_ref, *refs):
        dx_ref = refs[n_dp]
        step = pl.program_id(0)

        @pl.when(step == 0)
        def _():
            dx_ref[:, width:] = dw_ref[...]

        for piece in range(n_dp):

            @pl.when(step // count == piece)
            def _():
                start = (starts_ref[piece] + step - piece * count) * block
                dx_ref[:, pl.ds(pl.multiple_of(start, block), block)] = matmul(
                    dh_ref[...], refs[piece][...], BY_ROWS
                ).astype(bf16)

    def of_piece(piece):
        return lambda step, _: (jnp.clip(step - piece * count, 0, count - 1), 0)

    def whole(step, _):
        return (0, 0)

    return pl.pallas_call(
        kernel,
        out_shape=jax.ShapeDtypeStruct((slots, width + 128), bf16),
        grid_spec=pltpu.PrefetchScalarGridSpec(
            num_scalar_prefetch=1,
            grid=(n_dp * count,),
            in_specs=[
                pl.BlockSpec((slots, hidden_units), whole),
                pl.BlockSpec((slots, 128), whole),
            ]
            + [pl.BlockSpec((block, hidden_units), of_piece(piece)) for piece in range(n_dp)],
            out_specs=pl.BlockSpec((slots, width + 128), whole),
        ),
        compiler_params=pltpu.CompilerParams(vmem_limit_bytes=56 * 2**20),
        cost_estimate=pl.CostEstimate(
            flops=2 * slots * width * hidden_units,
            bytes_accessed=4 * slots * width,
            transcendentals=0,
        ),
        name="input_gradient",
    )(starts // block, dh, dw, *pieces)


def gradient_and_adam(start, routed, act, dh, received, state, first, second):
    slots = routed.shape[0]
    width = routed.shape[1] // 2
    part, both_hidden = state.shape[1:]
    hidden_units = both_hidden // 2
    block = min(256, part)

    def kernel(start_ref, x_ref, g_ref, act_ref, dh_ref, *refs):
        part_refs = refs[: len(received)]
        w_ref, m_ref, v_ref, w2_ref, m2_ref, v2_ref = refs[len(received) :]
        for half, (rows_ref, other_ref) in enumerate(((x_ref, dh_ref), (g_ref, act_ref))):
            cols = slice(half * hidden_units, (half + 1) * hidden_units)
            grad = matmul(rows_ref[...], other_ref[...], TRANSPOSED).astype(bf16).astype(f32)
            for part_ref in part_refs:
                grad = grad + part_ref[:, cols].astype(f32)
            new = adam_update(w_ref[0, :, cols], m_ref[0, :, cols], v_ref[0, :, cols], grad)
            for ref, value in zip((w2_ref, m2_ref, v2_ref), new):
                ref[0, :, cols] = value

    state_spec = pl.BlockSpec((1, block, both_hidden), lambda i, _: (0, i, 0))
    part_spec = pl.BlockSpec((block, both_hidden), lambda i, _: (i, 0))
    whole_spec = pl.BlockSpec((slots, hidden_units), lambda i, _: (0, 0))
    return pl.pallas_call(
        kernel,
        out_shape=[jax.ShapeDtypeStruct(state.shape, bf16)] * 3,
        grid_spec=pltpu.PrefetchScalarGridSpec(
            num_scalar_prefetch=1,
            grid=(part // block,),
            in_specs=[
                pl.BlockSpec((slots, block), lambda i, start_ref: (0, start_ref[0] + i)),
                pl.BlockSpec(
                    (slots, block), lambda i, start_ref: (0, width // block + start_ref[0] + i)
                ),
                whole_spec,
                whole_spec,
            ]
            + [part_spec] * len(received)
            + [state_spec] * 3,
            out_specs=[state_spec] * 3,
        ),
        compiler_params=pltpu.CompilerParams(vmem_limit_bytes=56 * 2**20),
        cost_estimate=pl.CostEstimate(
            flops=4 * slots * part * hidden_units,
            bytes_accessed=92 * part * both_hidden,
            transcendentals=2 * part * both_hidden,
        ),
        name="gradient_and_adam",
    )(start // block, routed, routed, act, dh, *received, state, first, second)


def trade(arrays, swap_pair, beside, operands):
    lanes_count = lax.axis_size("expert")
    half = lanes_count // 2
    own = lax.axis_index("expert") % half
    lanes = jnp.arange(half, dtype=jnp.int32)
    own_flag = jnp.sum(jnp.where(lanes == own, swap_pair, 0))
    other_flag = jnp.sum(jnp.where(lanes == own ^ 2, swap_pair, 0))
    side = (own >> 1) & 1
    rows = arrays[0].shape[1]
    cut = rows * 9 // 16

    def permute(value, pairs):
        return lax.ppermute(value, "expert", pairs)

    def stay(values, operands):
        return values, beside(*operands)

    def both(values, operands):
        pairs = [(slot ^ half, slot) for slot in range(lanes_count)]
        return tuple(permute(value, pairs) for value in values), beside(*operands)

    def one(trading):
        def run(values, operands):
            mine = [slot for slot in range(lanes_count) if (slot >> 1) & 1 == trading]
            across = [(slot ^ half, slot) for slot in mine]
            aside = [(slot, slot ^ 2) for slot in mine]
            across_aside = [(slot ^ half ^ 2, slot ^ 2) for slot in mine]
            back = [(slot ^ 2, slot) for slot in mine]
            last = [permute(value[:, cut:], aside) for value in values]
            first = [permute(value[:, :cut], across) for value in values]
            last = [permute(value, across_aside) for value in last]
            last = [permute(value, back) for value in last]
            traded = tuple(
                jnp.where(side == trading, jnp.concatenate([top, bottom], 1), value)
                for top, bottom, value in zip(first, last, values)
            )
            return traded, beside(*operands)

        return run

    if half < 4:
        return lax.cond(own_flag == 1, both, stay, arrays, operands)
    pattern = jnp.where(own_flag == 1, jnp.where(other_flag == 1, 3, 1 + side), 0)
    pattern = jnp.where((own_flag == 0) & (other_flag == 1), 2 - side, pattern)
    return lax.switch(pattern, [stay, one(0), one(1), both], arrays, operands)


def shards(
    tokens,
    upstream,
    expert_ids,
    route_weight,
    placement,
    swap_pair,
    expert_state,
    first_moment,
    second_moment,
):
    lanes_count = lax.axis_size("expert")
    n_dp = lax.axis_size("dp")
    rows, top = expert_ids.shape
    width = tokens.shape[1]
    hidden_units = expert_state.shape[2] // 2
    capacity = 2 * rows * top // lanes_count
    slots = lanes_count * capacity
    part = width // n_dp
    dp = lax.axis_index("dp")

    def exchange(value):
        return lax.all_to_all(
            value.reshape(lanes_count, capacity, -1), "expert", split_axis=0, concat_axis=0, tiled=True
        ).reshape(slots, -1)

    def shift(value, step):
        return lax.ppermute(value, "dp", [(i, (i + step) % n_dp) for i in range(n_dp)])

    state = expert_state[0]
    pieces = [state] + [shift(state, step) for step in range(1, n_dp)]
    starts = ((dp - jnp.arange(n_dp, dtype=jnp.int32)) % n_dp) * part

    rows_of_slots, position = dispatch(
        expert_ids.T, route_weight.T, placement, tokens, upstream, capacity
    )
    routed = exchange(rows_of_slots)
    act, dh, dw, *parts = expert_step(starts, routed, pieces)
    received = [shift(value, n_dp - step) for step, value in enumerate(parts, 1)]
    returned = exchange(input_gradient(starts, dh, dw, pieces))
    updated = gradient_and_adam(
        starts[:1], routed, act, dh, received, expert_state, first_moment, second_moment
    )

    def combine(returned, position, route_weight):
        slot = jnp.arange(slots, dtype=jnp.int32)
        hot = (slot[None, :, None] == position[:, None, :]).astype(bf16)
        token_grad = matmul(jnp.sum(hot, 0), returned[:, :width], TRANSPOSED).astype(bf16)
        dw_cols = matmul(hot, returned[:, width:], (((1,), (0,)), ((), ())))
        return token_grad, (dw_cols[:, :, 0].T / route_weight.astype(f32)).astype(bf16)

    updated, gradients = trade(
        tuple(updated), swap_pair, combine, (returned, position, route_weight)
    )
    return (*gradients, *updated)


def solution(mesh):
    in_specs = (
        P(("expert", "dp"), None),
        P(("expert", "dp"), None),
        P(("expert", "dp"), None),
        P(("expert", "dp"), None),
        P(),
        P(),
        P("expert", "dp", None),
        P("expert", "dp", None),
        P("expert", "dp", None),
    )
    out_specs = (
        P(("expert", "dp"), None),
        P(("expert", "dp"), None),
        P("expert", "dp", None),
        P("expert", "dp", None),
        P("expert", "dp", None),
    )
    return jax.shard_map(shards, mesh=mesh, in_specs=in_specs, out_specs=out_specs, check_vma=False)
```

```python
import math

import jax
import jax.numpy as jnp
from jax import lax
from jax.experimental import pallas as pl
from jax.experimental.pallas import tpu as pltpu
from jax.sharding import PartitionSpec as P

corr_one = 1.0 - math.exp(1000.0 * math.log(0.9))
corr_two = 1.0 - math.exp(1000.0 * math.log(0.999))

f32 = jnp.float32
bf16 = jnp.bfloat16


TRANSPOSED = (((0,), (0,)), ((), ()))
BY_ROWS = (((1,), (1,)), ((), ()))


def matmul(a, b, dims=(((1,), (0,)), ((), ()))):
    return lax.dot_general(a, b, dims, preferred_element_type=f32)


def adam_update(weights, first, second, grad):
    m_next = 0.9 * first.astype(f32) + 0.1 * grad
    v_next = 0.999 * second.astype(f32) + 0.001 * grad * grad
    root = v_next * (1.0 / corr_two)
    update = m_next * (1.0 / corr_one) / (root * lax.rsqrt(root) + 1e-08)
    w_old = weights.astype(f32)
    w_next = w_old - 0.001 * (update + 0.1 * w_old)
    return w_next.astype(bf16), m_next.astype(bf16), v_next.astype(bf16)


def dispatch(expert_ids, route_weight, placement, tokens, upstream, capacity):
    top, rows = expert_ids.shape
    lanes_count = placement.shape[0]
    slots = lanes_count * capacity
    width = tokens.shape[1]
    block = 512
    count = width // block

    def kernel(placement_ref, ids_ref, weight_ref, tokens_ref, upstream_ref, out_ref, position_ref, both_ref, weighted_ref):
        step = pl.program_id(0)

        @pl.when(step == 0)
        def _():
            ids = [ids_ref[k : k + 1, :] for k in range(top)]
            spread = [jnp.broadcast_to(row.astype(f32), (rows, rows)) for row in ids]
            earlier = lax.broadcasted_iota(jnp.int32, (rows, rows), 0) < lax.broadcasted_iota(
                jnp.int32, (rows, rows), 1
            )
            place = lax.broadcasted_iota(jnp.int32, (slots, rows), 0)
            both = jnp.zeros((slots, rows), f32)
            weighted = jnp.zeros((slots, rows), f32)
            for k in range(top):
                slot = jnp.zeros((1, rows), f32)
                for other in range(top):
                    same = (spread[other].T == spread[k]) & earlier
                    slot = slot + jnp.sum(jnp.where(same, 1.0, 0.0), 0, keepdims=True)
                dest = jnp.zeros((1, rows), jnp.int32)
                for expert in range(lanes_count):
                    dest = jnp.where(ids[k] == expert, placement_ref[expert], dest)
                position = dest * capacity + slot.astype(jnp.int32)
                position_ref[k : k + 1, :] = position
                hot = place == position
                both = jnp.where(hot, 1.0, both)
                weighted = jnp.where(hot, weight_ref[k : k + 1, :].astype(f32), weighted)
            both_ref[...] = both.astype(bf16)
            weighted_ref[...] = weighted.astype(bf16)

        @pl.when(step < count)
        def _():
            out_ref[...] = matmul(both_ref[...], tokens_ref[...]).astype(bf16)

        @pl.when(step >= count)
        def _():
            out_ref[...] = matmul(weighted_ref[...], upstream_ref[...]).astype(bf16)

    return pl.pallas_call(
        kernel,
        out_shape=[
            jax.ShapeDtypeStruct((slots, 2 * width), bf16),
            jax.ShapeDtypeStruct((top, rows), jnp.int32),
        ],
        grid_spec=pltpu.PrefetchScalarGridSpec(
            num_scalar_prefetch=1,
            grid=(2 * count,),
            in_specs=[
                pl.BlockSpec((top, rows), lambda i, _: (0, 0)),
                pl.BlockSpec((top, rows), lambda i, _: (0, 0)),
                pl.BlockSpec((rows, block), lambda i, _: (0, jnp.minimum(i, count - 1))),
                pl.BlockSpec((rows, block), lambda i, _: (0, jnp.maximum(i - count, 0))),
            ],
            out_specs=[
                pl.BlockSpec((slots, block), lambda i, _: (0, i)),
                pl.BlockSpec((top, rows), lambda i, _: (0, 0)),
            ],
            scratch_shapes=[pltpu.VMEM((slots, rows), bf16)] * 2,
        ),
        compiler_params=pltpu.CompilerParams(vmem_limit_bytes=56 * 2**20),
        cost_estimate=pl.CostEstimate(
            flops=4 * slots * rows * width, bytes_accessed=5 * slots * width, transcendentals=0
        ),
        name="dispatch",
    )(placement, expert_ids, route_weight, tokens, upstream)


def expert_step(starts, routed, pieces):
    slots = routed.shape[0]
    width = routed.shape[1] // 2
    n_dp = len(pieces)
    part, both_hidden = pieces[0].shape
    hidden_units = both_hidden // 2
    block = min(512, part)
    count = part // block
    total = n_dp * count

    def kernel(starts_ref, x_ref, g_ref, *refs):
        w_refs = refs[:n_dp]
        act_ref, dh_ref, dw_ref = refs[n_dp : n_dp + 3]
        part_refs = refs[n_dp + 3 : 2 * n_dp + 2]
        hid_ref, back_ref = refs[2 * n_dp + 2 :]
        step = pl.program_id(0)
        for piece in range(n_dp):

            @pl.when((step >= piece * count) & (step < (piece + 1) * count))
            def _():
                hid = matmul(x_ref[...], w_refs[piece][:, :hidden_units])
                back = matmul(g_ref[...], w_refs[piece][:, hidden_units:])

                @pl.when(step == 0)
                def _():
                    hid_ref[...] = hid
                    back_ref[...] = back

                @pl.when(step > 0)
                def _():
                    hid_ref[...] += hid
                    back_ref[...] += back

            if piece > 0:
                first = total + (piece - 1) * count

                @pl.when((step >= first) & (step < first + count))
                def _():
                    out = part_refs[piece - 1]
                    out[:, :hidden_units] = matmul(x_ref[...], dh_ref[...], TRANSPOSED).astype(bf16)
                    out[:, hidden_units:] = matmul(g_ref[...], act_ref[...], TRANSPOSED).astype(bf16)

        @pl.when(step == total - 1)
        def _():
            hid, back = hid_ref[...], back_ref[...]
            sig = jax.nn.sigmoid(hid)
            act = (hid * sig).astype(bf16)
            act_ref[...] = act
            dh_ref[...] = (back * (sig * (1.0 + hid * (1.0 - sig)))).astype(bf16)
            dw = jnp.sum(act.astype(f32) * back, 1, keepdims=True)
            dw_ref[...] = jnp.broadcast_to(dw, (slots, 128)).astype(bf16)

    def column(first):
        def index(step, starts_ref):
            at = jnp.where(step < total, step, step - total + count)
            return (0, first + starts_ref[at // count] + at % count)

        return index

    def of_piece(piece):
        return lambda step, _: (jnp.clip(step - piece * count, 0, count - 1), 0)

    def of_part(piece):
        return lambda step, _: (jnp.clip(step - total - (piece - 1) * count, 0, count - 1), 0)

    def whole(step, _):
        return (0, 0)

    return pl.pallas_call(
        kernel,
        out_shape=[
            jax.ShapeDtypeStruct((slots, hidden_units), bf16),
            jax.ShapeDtypeStruct((slots, hidden_units), bf16),
            jax.ShapeDtypeStruct((slots, 128), bf16),
        ]
        + [jax.ShapeDtypeStruct((part, both_hidden), bf16)] * (n_dp - 1),
        grid_spec=pltpu.PrefetchScalarGridSpec(
            num_scalar_prefetch=1,
            grid=(total + (n_dp - 1) * count,),
            in_specs=[
                pl.BlockSpec((slots, block), column(0)),
                pl.BlockSpec((slots, block), column(width // block)),
            ]
            + [pl.BlockSpec((block, both_hidden), of_piece(piece)) for piece in range(n_dp)],
            out_specs=[
                pl.BlockSpec((slots, hidden_units), whole),
                pl.BlockSpec((slots, hidden_units), whole),
                pl.BlockSpec((slots, 128), whole),
            ]
            + [pl.BlockSpec((block, both_hidden), of_part(piece)) for piece in range(1, n_dp)],
            scratch_shapes=[pltpu.VMEM((slots, hidden_units), f32)] * 2,
        ),
        compiler_params=pltpu.CompilerParams(vmem_limit_bytes=48 * 2**20),
        cost_estimate=pl.CostEstimate(
            flops=8 * slots * width * hidden_units,
            bytes_accessed=16 * slots * width,
            transcendentals=slots * hidden_units,
        ),
        name="expert_step",
    )(starts // block, routed, routed, *pieces)


def input_gradient(starts, dh, dw, pieces):
    slots, hidden_units = dh.shape
    n_dp = len(pieces)
    part = pieces[0].shape[0]
    width = n_dp * part
    block = min(512, part)
    count = part // block

    def kernel(starts_ref, dh_ref, dw_ref, *refs):
        dx_ref = refs[n_dp]
        step = pl.program_id(0)

        @pl.when(step == 0)
        def _():
            dx_ref[:, width:] = dw_ref[...]

        for piece in range(n_dp):

            @pl.when(step // count == piece)
            def _():
                start = (starts_ref[piece] + step - piece * count) * block
                dx_ref[:, pl.ds(pl.multiple_of(start, block), block)] = matmul(
                    dh_ref[...], refs[piece][...], BY_ROWS
                ).astype(bf16)

    def of_piece(piece):
        return lambda step, _: (jnp.clip(step - piece * count, 0, count - 1), 0)

    def whole(step, _):
        return (0, 0)

    return pl.pallas_call(
        kernel,
        out_shape=jax.ShapeDtypeStruct((slots, width + 128), bf16),
        grid_spec=pltpu.PrefetchScalarGridSpec(
            num_scalar_prefetch=1,
            grid=(n_dp * count,),
            in_specs=[
                pl.BlockSpec((slots, hidden_units), whole),
                pl.BlockSpec((slots, 128), whole),
            ]
            + [pl.BlockSpec((block, hidden_units), of_piece(piece)) for piece in range(n_dp)],
            out_specs=pl.BlockSpec((slots, width + 128), whole),
        ),
        compiler_params=pltpu.CompilerParams(vmem_limit_bytes=32 * 2**20),
        cost_estimate=pl.CostEstimate(
            flops=2 * slots * width * hidden_units,
            bytes_accessed=4 * slots * width,
            transcendentals=0,
        ),
        name="input_gradient",
    )(starts // block, dh, dw, *pieces)


def gradient_and_adam(start, routed, act, dh, received, state, first, second):
    slots = routed.shape[0]
    width = routed.shape[1] // 2
    part, both_hidden = state.shape[1:]
    hidden_units = both_hidden // 2
    block = min(256, part)

    def kernel(start_ref, x_ref, g_ref, act_ref, dh_ref, *refs):
        part_refs = refs[: len(received)]
        w_ref, m_ref, v_ref, w2_ref, m2_ref, v2_ref = refs[len(received) :]
        for half, (rows_ref, other_ref) in enumerate(((x_ref, dh_ref), (g_ref, act_ref))):
            cols = slice(half * hidden_units, (half + 1) * hidden_units)
            grad = matmul(rows_ref[...], other_ref[...], TRANSPOSED).astype(bf16).astype(f32)
            for part_ref in part_refs:
                grad = grad + part_ref[:, cols].astype(f32)
            new = adam_update(w_ref[0, :, cols], m_ref[0, :, cols], v_ref[0, :, cols], grad)
            for ref, value in zip((w2_ref, m2_ref, v2_ref), new):
                ref[0, :, cols] = value

    state_spec = pl.BlockSpec((1, block, both_hidden), lambda i, _: (0, i, 0))
    part_spec = pl.BlockSpec((block, both_hidden), lambda i, _: (i, 0))
    whole_spec = pl.BlockSpec((slots, hidden_units), lambda i, _: (0, 0))
    return pl.pallas_call(
        kernel,
        out_shape=[jax.ShapeDtypeStruct(state.shape, bf16)] * 3,
        grid_spec=pltpu.PrefetchScalarGridSpec(
            num_scalar_prefetch=1,
            grid=(part // block,),
            in_specs=[
                pl.BlockSpec((slots, block), lambda i, start_ref: (0, start_ref[0] + i)),
                pl.BlockSpec(
                    (slots, block), lambda i, start_ref: (0, width // block + start_ref[0] + i)
                ),
                whole_spec,
                whole_spec,
            ]
            + [part_spec] * len(received)
            + [state_spec] * 3,
            out_specs=[state_spec] * 3,
        ),
        compiler_params=pltpu.CompilerParams(vmem_limit_bytes=48 * 2**20),
        cost_estimate=pl.CostEstimate(
            flops=4 * slots * part * hidden_units,
            bytes_accessed=180 * part * both_hidden,
            transcendentals=2 * part * both_hidden,
        ),
        name="gradient_and_adam",
    )(start // block, routed, routed, act, dh, *received, state, first, second)


def trade(arrays, swap_pair, beside, operands):
    lanes_count = lax.axis_size("expert")
    half = lanes_count // 2
    own = lax.axis_index("expert") % half
    lanes = jnp.arange(half, dtype=jnp.int32)
    own_flag = jnp.sum(jnp.where(lanes == own, swap_pair, 0))
    other_flag = jnp.sum(jnp.where(lanes == own ^ 2, swap_pair, 0))
    side = (own >> 1) & 1
    rows = arrays[0].shape[1]
    cut = rows * 9 // 16

    def permute(value, pairs):
        return lax.ppermute(value, "expert", pairs)

    def stay(values, operands):
        return values, beside(*operands)

    def both(values, operands):
        pairs = [(slot ^ half, slot) for slot in range(lanes_count)]
        return tuple(permute(value, pairs) for value in values), beside(*operands)

    def one(trading):
        def run(values, operands):
            mine = [slot for slot in range(lanes_count) if (slot >> 1) & 1 == trading]
            across = [(slot ^ half, slot) for slot in mine]
            aside = [(slot, slot ^ 2) for slot in mine]
            across_aside = [(slot ^ half ^ 2, slot ^ 2) for slot in mine]
            back = [(slot ^ 2, slot) for slot in mine]
            last = [permute(value[:, cut:], aside) for value in values]
            first = []
            for value in values:
                top = value[:, :cut]
                if first:
                    top, first[-1] = lax.optimization_barrier((top, first[-1]))
                first.append(permute(top, across))
            last = [permute(value, across_aside) for value in last]
            last = [permute(value, back) for value in last]
            traded = tuple(
                jnp.where(side == trading, jnp.concatenate([top, bottom], 1), value)
                for top, bottom, value in zip(first, last, values)
            )
            return traded, beside(*operands)

        return run

    if half < 4:
        return lax.cond(own_flag == 1, both, stay, arrays, operands)
    pattern = jnp.where(own_flag == 1, jnp.where(other_flag == 1, 3, 1 + side), 0)
    pattern = jnp.where((own_flag == 0) & (other_flag == 1), 2 - side, pattern)
    return lax.switch(pattern, [stay, one(0), one(1), both], arrays, operands)


def shards(
    tokens,
    upstream,
    expert_ids,
    route_weight,
    placement,
    swap_pair,
    expert_state,
    first_moment,
    second_moment,
):
    lanes_count = lax.axis_size("expert")
    n_dp = lax.axis_size("dp")
    rows, top = expert_ids.shape
    width = tokens.shape[1]
    hidden_units = expert_state.shape[2] // 2
    capacity = 2 * rows * top // lanes_count
    slots = lanes_count * capacity
    part = width // n_dp
    dp = lax.axis_index("dp")

    def exchange(value):
        return lax.all_to_all(
            value.reshape(lanes_count, capacity, -1), "expert", split_axis=0, concat_axis=0, tiled=True
        ).reshape(slots, -1)

    def shift(value, step):
        return lax.ppermute(value, "dp", [(i, (i + step) % n_dp) for i in range(n_dp)])

    state = expert_state[0]
    pieces = [state] + [shift(state, step) for step in range(1, n_dp)]
    starts = ((dp - jnp.arange(n_dp, dtype=jnp.int32)) % n_dp) * part

    rows_of_slots, position = dispatch(
        expert_ids.T, route_weight.T, placement, tokens, upstream, capacity
    )
    routed = exchange(rows_of_slots)
    act, dh, dw, *parts = expert_step(starts, routed, pieces)
    received = [shift(value, n_dp - step) for step, value in enumerate(parts, 1)]
    returned = exchange(input_gradient(starts, dh, dw, pieces))
    updated = gradient_and_adam(
        starts[:1], routed, act, dh, received, expert_state, first_moment, second_moment
    )

    def combine(returned, position, route_weight):
        slot = jnp.arange(slots, dtype=jnp.int32)
        hot = (slot[None, :, None] == position[:, None, :]).astype(bf16)
        token_grad = matmul(jnp.sum(hot, 0), returned[:, :width], TRANSPOSED).astype(bf16)
        dw_cols = matmul(hot, returned[:, width:], (((1,), (0,)), ((), ())))
        return token_grad, (dw_cols[:, :, 0].T / route_weight.astype(f32)).astype(bf16)

    updated, gradients = trade(
        tuple(updated), swap_pair, combine, (returned, position, route_weight)
    )
    return (*gradients, *updated)


def solution(mesh):
    in_specs = (
        P(("expert", "dp"), None),
        P(("expert", "dp"), None),
        P(("expert", "dp"), None),
        P(("expert", "dp"), None),
        P(),
        P(),
        P("expert", "dp", None),
        P("expert", "dp", None),
        P("expert", "dp", None),
    )
    out_specs = (
        P(("expert", "dp"), None),
        P(("expert", "dp"), None),
        P("expert", "dp", None),
        P("expert", "dp", None),
        P("expert", "dp", None),
    )
    return jax.shard_map(shards, mesh=mesh, in_specs=in_specs, out_specs=out_specs, check_vma=False)
```
